128 devices in a mesh: row: 16 (over x, z_hi, core), col: 8 (over y, z_lo).
Axes of the slice: x: 4, y: 4, z: 4 (z_hi: 2, z_lo: 2; z = z_hi * 2 + z_lo), core: 2. Of those that a mesh axis runs over, the one named last changes fastest.
Arguments:
- tokens: bfloat16 [2, 256, 384, 512], P(None, 'row', 'col'), may hold values from -8 to 8
- region: int32 [256, 384], P('row', 'col'), may hold values from 0 to 2, as said below
- w_qkv: bfloat16 [512, 1536], P(('row', 'col')), may hold values from -0.25 to 0.25
- w_proj: bfloat16 [512, 512], P(('row', 'col')), may hold values from -0.25 to 0.25
- w_fc1: bfloat16 [512, 2048], P(('row', 'col')), may hold values from -0.25 to 0.25
- w_fc2: bfloat16 [2048, 512], P(('row', 'col')), may hold values from -0.125 to 0.125
- gain_attn: float32 [512], replicated, may hold values from 0.5 to 1.5
- gain_mlp: float32 [512], replicated, may hold values from 0.5 to 1.5
- table: float32 [961, 16], replicated, may hold values from -4 to 4
- index: int32 [256, 256], replicated, may hold values from 0 to 960
- logit_scale: float32 [16], replicated, may hold values from 3 to 10
Outputs:
- block_out: bfloat16 [2, 256, 384, 512], P(None, 'row', 'col')
The draws below stay inside these ranges and needn't reach their ends.
Inputs may be any that keep to these rules, and one draw needn't show every extreme that they name: The shifted grid falls into nine regions: rows before 256 - 16, rows from there before 256 - 8, and the last 8 rows, crossed with the same three parts of the columns; all positions of one region share a label, and each label is that of exactly three regions.
All inputs are finite; a program needn't handle non-finite values.
Results may differ from the reference program's by a relative error of at most 0.02.
Values may be sent and summed in bfloat16 or wider, within the bound.
A program may use at most 128 MiB of HBM per device.

```python
import math
import jax
import jax.numpy as jnp
from jax import lax

DIM = 512
HEADS = 16
MLP_DIM = 2048
WINDOW = 16
SHIFT = 8
IMAGES = 2
HEIGHT = 256
WIDTH = 384
TABLE_ROWS = 961
LTOK = 256


def draw_tokens(key, part):
    key = jax.random.fold_in(key, 5)
    base_key, scale_key = jax.random.split(key)
    base = jnp.clip(jax.random.normal(base_key, (IMAGES, HEIGHT, WIDTH, DIM), jnp.float32), -4.0, 4.0)
    log_scale = jax.random.uniform(scale_key, (IMAGES, HEIGHT, WIDTH, 1), jnp.float32, math.log(0.05), math.log(2.0))
    return (base * jnp.exp(log_scale)).astype(jnp.bfloat16)


def draw_region(key, part):
    key = jax.random.fold_in(key, 11)
    labels = (jax.random.permutation(key, 9) % 3).astype(jnp.int32)
    rows = jnp.arange(HEIGHT, dtype=jnp.int32)
    cols = jnp.arange(WIDTH, dtype=jnp.int32)
    row_part = (rows >= HEIGHT - WINDOW).astype(jnp.int32) + (rows >= HEIGHT - SHIFT).astype(jnp.int32)
    col_part = (cols >= WIDTH - WINDOW).astype(jnp.int32) + (cols >= WIDTH - SHIFT).astype(jnp.int32)
    which = 3 * row_part[:, None] + col_part[None, :]
    picks = (which[:, :, None] == jnp.arange(9, dtype=jnp.int32)[None, None, :]).astype(jnp.int32)
    return jnp.sum(picks * labels[None, None, :], -1).astype(jnp.int32)


def with_ends(result, key, least, top_value):
    longest = result.shape.index(max(result.shape))
    spots = []
    for shift in (0, 1):
        where = [jax.random.randint(jax.random.fold_in(key, axis), (), 0, length) for axis, length in enumerate(result.shape)]
        where[longest] = (where[longest] + shift) % result.shape[longest]
        spots.append(tuple(where))
    return result.at[spots[0]].set(least).at[spots[1]].set(top_value)


def shard_levels(stream_key, dims, cuts, least, largest):
    def one(dim, shards_of):
        steps = jax.random.uniform(jax.random.fold_in(jax.random.fold_in(stream_key, 6), dim), (shards_of,), jnp.float32, least / len(cuts), largest / len(cuts))
        return jnp.repeat(jnp.exp(steps), dims[dim] // shards_of).reshape((-1,) + (1,) * (len(dims) - dim - 1))

    level = one(*cuts[0])
    for cut in cuts[1:]:
        level = level * one(*cut)
    return level


def noise(stream_key, extent, scale, bound, pieces=(), kind=jnp.bfloat16):
    values = jax.random.normal(stream_key, extent, jnp.float32) * scale
    if len(pieces) > 0:
        values = shard_levels(stream_key, extent, pieces, -0.22, 0.18) * values
    return jnp.clip(values, min=-bound, max=bound).astype(kind)


def setup_inputs(seed: int = 0) -> dict:
    splits = jax.random.split(jax.random.key(seed), 12)
    return {
        "tokens": draw_tokens(jax.random.fold_in(splits[11], 71), 0),
        "region": draw_region(jax.random.fold_in(splits[11], 71), 0),
        "w_qkv": noise(splits[2], (DIM, 3 * DIM), DIM ** -0.5, 0.25, ((0, 128),)),
        "w_proj": noise(splits[3], (DIM, DIM), DIM ** -0.5, 0.25, ((0, 128),)),
        "w_fc1": noise(splits[4], (DIM, MLP_DIM), DIM ** -0.5, 0.25, ((0, 128),)),
        "w_fc2": noise(splits[5], (MLP_DIM, DIM), MLP_DIM ** -0.5, 0.125, ((0, 128),)),
        "gain_attn": jnp.clip(1.0 + 0.1 * jax.random.normal(splits[6], (DIM,), jnp.float32), 0.5, 1.5),
        "gain_mlp": jnp.clip(1.0 + 0.1 * jax.random.normal(splits[7], (DIM,), jnp.float32), 0.5, 1.5),
        "table": noise(splits[8], (TABLE_ROWS, HEADS), 1.0, 4.0, (), jnp.float32),
        "index": with_ends(jax.random.randint(splits[9], (LTOK, LTOK), 0, TABLE_ROWS), jax.random.fold_in(splits[9], 1), 0, TABLE_ROWS - 1).astype(jnp.int32),
        "logit_scale": jnp.clip(jnp.exp(jax.random.uniform(splits[10], (HEADS,), jnp.float32, math.log(3.0), math.log(10.0))), 3.0, 10.0),
    }


def unit_length(vectors):
    return vectors / jnp.maximum(jnp.sqrt(lax.optimization_barrier(jnp.sum(vectors * vectors, -1, keepdims=True))), 1.0)

def normed(value, gain):
    mean_val = lax.optimization_barrier(jnp.mean(value, -1, keepdims=True))
    centered = value - mean_val
    variance = lax.optimization_barrier(jnp.mean(centered * centered, -1, keepdims=True))
    return centered * lax.rsqrt(variance + 1e-05) * gain

def position_bias(table, index):
    return jnp.transpose(16.0 * jax.nn.sigmoid(table[index]), (2, 0, 1))

def windowed(tile_in, labels_tile, side):
    images, tile_rows, tile_cols, channels = tile_in.shape
    blocks = tile_in.reshape(images, tile_rows // side, side, tile_cols // side, side, channels)
    blocks = blocks.transpose(0, 1, 3, 2, 4, 5).reshape(-1, side * side, channels)
    labels = labels_tile.reshape(tile_rows // side, side, tile_cols // side, side)
    labels = labels.transpose(0, 2, 1, 3).reshape(-1, side * side)
    return (blocks, jnp.tile(labels, (images, 1)))

def unwindow(blocks, images, tile_rows, tile_cols, side):
    channels = blocks.shape[-1]
    grid = blocks.reshape(images, tile_rows // side, tile_cols // side, side, side, channels)
    return grid.transpose(0, 1, 3, 2, 4, 5).reshape(images, tile_rows, tile_cols, channels)

def attention(blocks, labels, w_qkv, w_proj, pos_bias, logit_scale):
    num_windows, win_length, channels = blocks.shape
    projected = jnp.dot(blocks.reshape(num_windows * win_length, channels), w_qkv, preferred_element_type=jnp.float32).astype(jnp.bfloat16)
    projected = projected.reshape(num_windows, win_length, 3, HEADS, channels // HEADS)
    queries = unit_length(projected[:, :, 0].astype(jnp.float32))
    key_unit = unit_length(projected[:, :, 1].astype(jnp.float32))
    values = projected[:, :, 2].astype(jnp.float32)
    cosine = jnp.einsum('wqhd,wkhd->whqk', queries, key_unit)
    same_region = labels[:, :, None] == labels[:, None, :]
    mask_add = jnp.where(same_region, 0.0, -100.0).astype(jnp.float32)
    scores = cosine * logit_scale[None, :, None, None] + pos_bias[None] + mask_add[:, None]
    exponent = jnp.exp(scores)
    weights = (exponent / lax.optimization_barrier(jnp.sum(exponent, -1, keepdims=True))).astype(jnp.bfloat16)
    mixed_heads = jnp.einsum('whqk,wkhd->wqhd', weights.astype(jnp.float32), values).astype(jnp.bfloat16)
    mixed_heads = mixed_heads.reshape(num_windows * win_length, channels)
    return jnp.dot(mixed_heads, w_proj, preferred_element_type=jnp.float32).astype(jnp.bfloat16).reshape(num_windows, win_length, channels)

def finish_block(tokens_flat, attended, w_fc1, w_fc2, gain_attn, gain_mlp):
    after_attn = (tokens_flat.astype(jnp.float32) + normed(attended.astype(jnp.float32), gain_attn)).astype(jnp.bfloat16)
    hidden = jax.nn.gelu(jnp.dot(after_attn, w_fc1, preferred_element_type=jnp.float32), approximate=False).astype(jnp.bfloat16)
    mlp_out = jnp.dot(hidden, w_fc2, preferred_element_type=jnp.float32)
    return (after_attn.astype(jnp.float32) + normed(mlp_out, gain_mlp)).astype(jnp.bfloat16)

def reference(tokens, region, w_qkv, w_proj, w_fc1, w_fc2, gain_attn, gain_mlp, table, index, logit_scale):
    rolled = jnp.roll(tokens, (-SHIFT, -SHIFT), (1, 2))
    band_count = HEIGHT // WINDOW
    bands = rolled.reshape(IMAGES * band_count, WINDOW, WIDTH, DIM)
    region_bands = jnp.tile(region.reshape(band_count, WINDOW, WIDTH), (IMAGES, 1, 1))
    pos_bias = position_bias(table, index)

    def one_band(pair_in):
        band_in, labels_band = pair_in
        blocks, labels = windowed(band_in[None], labels_band, WINDOW)
        mixed_out = attention(blocks, labels, w_qkv, w_proj, pos_bias, logit_scale)
        return unwindow(mixed_out, 1, WINDOW, WIDTH, WINDOW)[0]
    attended = lax.map(one_band, (bands, region_bands)).reshape(IMAGES, HEIGHT, WIDTH, DIM)
    attended = jnp.roll(attended, (SHIFT, SHIFT), (1, 2))

    def mlp_band(pair_in):
        return finish_block(pair_in[0], pair_in[1], w_fc1, w_fc2, gain_attn, gain_mlp)
    flat_tokens = tokens.reshape(IMAGES * band_count, WINDOW * WIDTH, DIM)
    flat_attended = attended.reshape(IMAGES * band_count, WINDOW * WIDTH, DIM)
    block_out = lax.map(mlp_band, (flat_tokens, flat_attended))
    return block_out.reshape(IMAGES, HEIGHT, WIDTH, DIM)
```

```python
import math

import jax
import jax.numpy as jnp
from jax import lax
from jax.experimental import pallas as pl
from jax.experimental.pallas import tpu as pltpu
from jax.sharding import PartitionSpec as P

MESH = pl.DeviceIdType.MESH
BF = jnp.bfloat16
F32 = jnp.float32
LOG2E = math.log2(math.e)
ROUTES = ((1, 2, 0), (2, 0, 1), (0, 1, 2))


def iota(shape, dim):
    return lax.broadcasted_iota(jnp.int32, shape, dim)


def layer_norm(value, gain):
    mean = jnp.mean(value, -1, keepdims=True)
    centered = value - mean
    variance = jnp.mean(centered * centered, -1, keepdims=True)
    return centered * lax.rsqrt(variance + 1e-05) * gain


def own_block(w_ref, lo, lanes, tmp):
    for quarter in range(4):
        at = lo + quarter * lanes
        tmp[4 * quarter : 4 * quarter + 4, :lanes] = w_ref[:, at : at + lanes].astype(F32)
    return tmp[:, :lanes].astype(BF)


def kernel(
    tok_hbm, region_ref, wqkv_ref, wproj_ref, wfc1_ref, wfc2_ref,
    gain1_ref, gain2_ref, table_ref, index_ref, scale_ref,
    out_hbm,
    raw, T, X, A, R, O, GQ, GP, G1, G2, WQ, WP, W1, W2,
    QKV, M, bias, tab, RS, RT, LB, FQ, FK, tmp,
    raw_sem, out_sem, g_send, g_recv, d_send, d_recv, h_send, h_recv, r_send, r_recv,
):
    row, col = lax.axis_index("row"), lax.axis_index("col")
    core = lax.rem(row, 2)
    at = (row // 4, col // 2, lax.rem(row // 2, 2) * 2 + lax.rem(col, 2))

    def chip(x, y, z, c):
        return {"row": x * 4 + (z // 2) * 2 + c, "col": y * 2 + lax.rem(z, 2)}

    def near(dr, dc):
        return {"row": lax.rem(row + dr + 16, 16), "col": lax.rem(col + dc + 8, 8)}

    def along(axis, step):
        spot = list(at)
        spot[axis] = lax.rem(spot[axis] + step, 4)
        return chip(*spot, core)

    sibling = chip(*at, 1 - core)
    loads = [pltpu.make_async_copy(tok_hbm.at[i], raw.at[i], raw_sem.at[i]) for i in range(2)]
    for copy in loads:
        copy.start()

    peers = [along(axis, step) for axis in range(3) for step in (1, 2, 3)] + [sibling]
    peers += [near(-1, 0), near(1, 0), near(0, -1), near(0, 1), near(-1, -1), near(1, 1)]
    barrier = pltpu.get_barrier_semaphore()
    for peer in peers:
        pl.semaphore_signal(barrier, inc=1, device_id=peer, device_id_type=MESH)

    for flow in range(3):
        GQ[flow, core, at[0], at[1], at[2]] = own_block(wqkv_ref, 512 * flow, 128, tmp)
    GP[core, at[0], at[1], at[2]] = own_block(wproj_ref, 0, 128, tmp)
    G1[core, at[0], at[1], at[2]] = own_block(wfc1_ref, 0, 512, tmp)
    G2[core, at[0], at[1], at[2]] = wfc2_ref[...]
    RS[0] = jnp.zeros((16, 128), jnp.int32)
    RS[0, :, 0:48] = region_ref[...]

    pl.semaphore_wait(barrier, len(peers))

    sends = []

    def send(src, dst, s_sem, r_sem, device):
        copy = pltpu.make_async_remote_copy(
            src_ref=src, dst_ref=dst, send_sem=s_sem, recv_sem=r_sem,
            device_id=device, device_id_type=MESH,
        )
        copy.start()
        sends.append(copy)
        return copy

    batches = ([GQ.at[0], GQ.at[1], GQ.at[2]], [G1, G2, GP])

    def slab(batch, flow, known, axis=None, step=0):
        spot = list(at)
        if axis is not None:
            spot[axis] = lax.rem(spot[axis] + step, 4)
        pick = tuple(slice(None) if a in known else spot[a] for a in range(3))
        return batches[batch][flow].at[(core,) + pick]

    def gather_step(batch, step):
        copies = []
        for flow in range(3):
            route = ROUTES[flow]
            part = slab(batch, flow, route[:step])
            copies.append([
                send(part, part, g_send.at[batch, flow, step, t - 1], g_recv.at[batch, flow, step, t - 1],
                     along(route[step], t))
                for t in (1, 3, 2)
            ])
        return copies

    def across(batch, flow, piece):
        route = ROUTES[flow]
        part = slab(batch, flow, route[:2], route[2], piece)
        return send(part, part, d_send.at[batch, flow, piece], d_recv.at[batch, flow, piece], sibling)

    def await_all(copies):
        for group in copies:
            for copy in group:
                copy.wait_recv()

    def last_step(batch):
        final = gather_step(batch, 2)
        crossed = [across(batch, flow, 0) for flow in range(3)]
        return final, crossed

    def finish(batch, final, crossed):
        for order, piece in enumerate((3, 1, 2)):
            for flow in range(3):
                final[flow][order].wait_recv()
                crossed.append(across(batch, flow, piece))
        return crossed

    first = gather_step(0, 0)

    halo = [
        send(RS.at[0], RS.at[1], h_send.at[6], h_recv.at[6], near(1, 0)),
        send(RS.at[0], RS.at[2], h_send.at[7], h_recv.at[7], near(1, 1)),
    ]
    for image in range(2):
        loads[image].wait()
        for half in (image, 1 - image):
            rows = raw[image, 8 * half : 8 * half + 8].astype(F32)
            for group in range(6):
                part = rows[:, 8 * group : 8 * group + 8, :].reshape(64, 512).astype(BF)
                T[image, half, group] = part
                if image == 0 and half == 1 and group > 0:
                    X[0, 0, group - 1] = part
                if image == 1 and half == 0 and group < 5:
                    X[1, 1, group + 1] = part
        if image == 0:
            halo.append(send(T.at[0, 0, 1:6], X.at[0, 1, 0:5], h_send.at[0], h_recv.at[0], near(-1, 0)))
            halo.append(send(T.at[0, 0, 0], X.at[0, 1, 5], h_send.at[1], h_recv.at[1], near(-1, -1)))
            halo.append(send(T.at[0, 1, 0], X.at[0, 0, 5], h_send.at[2], h_recv.at[2], near(0, -1)))
        else:
            halo.append(send(T.at[1, 1, 0:5], X.at[1, 0, 1:6], h_send.at[3], h_recv.at[3], near(1, 0)))
            halo.append(send(T.at[1, 1, 5], X.at[1, 0, 0], h_send.at[4], h_recv.at[4], near(1, 1)))
            halo.append(send(T.at[1, 0, 5], X.at[1, 1, 0], h_send.at[5], h_recv.at[5], near(0, 1)))

    await_all(first)
    second = gather_step(0, 1)

    for chunk in range(8):
        base = 128 * chunk if chunk < 7 else 961 - 128
        tab[chunk] = (16.0 * LOG2E) * jax.nn.sigmoid(table_ref[base : base + 128, :].T)
    lane = iota((8, 128), 1)
    reorder = (lane // 8 % 8) * 16 + (lane // 64) * 8 + lane % 8

    def bias_rows(start, stop):
        def one(n, carry):
            source = (n // 16) * 128 + (n % 8) * 16 + (n // 8 % 2) * 8
            for half in range(2):
                index = index_ref[pl.ds(pl.multiple_of(source, 8), 8), 128 * half : 128 * half + 128]
                index = jnp.take_along_axis(index, reorder, axis=1, mode="promise_in_bounds")
                high = index // 128
                low = jnp.where(high == 7, index - (961 - 128), index % 128)
                for head in range(16):
                    found = jnp.zeros((8, 128), F32)
                    for chunk in range(8):
                        entry = jnp.broadcast_to(tab[chunk, head : head + 1, :], (8, 128))
                        value = jnp.take_along_axis(entry, low, axis=1, mode="promise_in_bounds")
                        found = jnp.where(high == chunk, value, found)
                    bias[head, pl.ds(pl.multiple_of(n * 8, 8), 8), 128 * half : 128 * half + 128] = found
            return carry

        lax.fori_loop(start, stop, one, 0)

    bias_rows(0, 16)
    await_all(second)
    final, crossed = last_step(0)
    other = gather_step(1, 0)
    bias_rows(16, 32)

    for copy in halo[:2]:
        copy.wait_recv()
    for place in range(3):
        RT[place] = RS[place].astype(F32).T

    crossed = finish(0, final, crossed)
    await_all(other)
    other = gather_step(1, 1)

    o, i = iota((256, 256), 0), iota((256, 256), 1)
    spot = (o // 8 % 4) * 64 + (o // 32 % 2) * 32 + (o // 4 % 2) * 16 + (o // 64) * 4 + o % 4
    permute = jnp.where(spot == i, 1.0, 0.0).astype(BF)
    squares = jnp.where(o // 32 == i // 32, 1.0, 0.0).astype(BF)

    def natural(source, dest, lanes):
        def one(n, carry):
            c, x = n // 4, n % 4
            found = jnp.dot(permute, source[c, x].reshape(256, lanes), preferred_element_type=F32).astype(BF)
            for quarter in range(4):
                for high in range(2):
                    base = 64 * quarter + 32 * high
                    to = pl.multiple_of(x * 128 + high * 64 + c * 32, 32)
                    dest[pl.ds(to, 32), lanes * quarter : lanes * quarter + lanes] = found[base : base + 32]
            return carry

        lax.fori_loop(0, 8, one, 0)

    for copy in crossed:
        copy.wait_recv()
    for flow in range(3):
        natural(GQ.at[flow], WQ.at[flow], 128)
    for copy in halo[2:]:
        copy.wait_recv()

    lane512 = iota((1, 512), 1)
    scale = jnp.zeros((1, 512), F32)
    for head in range(16):
        scale = jnp.where(lane512 // 32 == head, scale_ref[head] * LOG2E, scale)

    def project(w, carry):
        image, j = w // 3, w % 3
        x = X[image, :, pl.ds(2 * j, 2)].reshape(256, 512)
        for kind in range(3):
            value = jnp.dot(x, WQ[kind], preferred_element_type=F32)
            if kind < 2:
                square = (value * value).astype(BF)
                length = jnp.concatenate(
                    [jnp.dot(square[:, 256 * s : 256 * s + 256], squares, preferred_element_type=F32) for s in range(2)], 1)
                unit = lax.rsqrt(jnp.maximum(length, 1.0))
                value = value * (unit * scale if kind == 0 else unit)
            value = value.astype(BF)
            for block in range(4):
                QKV[w, kind, block] = value[:, 128 * block : 128 * block + 128]
        return carry

    lax.fori_loop(0, 6, project, 0)
    await_all(other)
    final, crossed = last_step(1)

    lane128 = iota((1, 128), 1)
    ones = jnp.ones((256, 128), BF)

    def attend(image, j):
        w = 3 * image + j
        place, start = (0, 16 * j) if image == 0 else ((2, 32) if j == 0 else (1, 16 * (j - 1)))
        for n in range(32):
            a, b = (n // 16) * 8 + n % 8, n // 8 % 2
            LB[8 * n : 8 * n + 8] = jnp.broadcast_to(RT[place, start + 8 * b : start + 8 * b + 8, a : a + 1], (8, 128))
        label = LB[...]
        for i in range(4):
            m = lane128 - 32 * ((i + 1) % 4)
            target = jnp.where((m >= 0) & (m < 6), m % 3, -1).astype(F32)
            hi, lo = 144.0, 100.0 * LOG2E - 144.0
            big = jnp.where(m < 3, hi, lo)
            rest = jnp.where(m == 6, -hi, jnp.where(m == 7, -lo, 0.0))
            unit = jnp.where((m == 6) | (m == 7), 1.0, 0.0)
            same = label == target
            FQ[i] = jnp.where(same, big, rest).astype(BF)
            FK[i] = jnp.where(same, 1.0, unit).astype(BF)

        def heads(block, carry):
            q, k = QKV[w, 0, block], QKV[w, 1, block]
            v = jnp.concatenate([QKV[w, 2, block], ones], 1)
            top = jnp.zeros((256, 128), F32)
            total = jnp.zeros((256, 128), F32)
            for i in range(4):
                here = lane128 // 32 == i
                keep = jnp.where(here, 1.0, 0.0).astype(BF)
                qh = q * keep + FQ[i]
                kh = k * keep + FK[i]
                score = lax.dot_general(qh, kh, (((1,), (1,)), ((), ())), preferred_element_type=F32)
                weight = jnp.exp2(score + bias[4 * block + i]).astype(BF)
                found = jnp.dot(weight, v, preferred_element_type=F32)
                top = jnp.where(here, found[:, :128], top)
                total = jnp.where(here, found[:, 128:], total)
            M[block] = (top / total).astype(BF)
            return carry

        lax.fori_loop(0, 4, heads, 0)
        mixed = jnp.concatenate([M[b] for b in range(4)], 1)
        done = jnp.dot(mixed, WP[...], preferred_element_type=F32).astype(BF).reshape(2, 2, 64, 512)
        for upper in range(2):
            for right in range(2):
                g = 2 * j + right
                if image == 0 and upper == 0 and g < 5:
                    R[0, 1, g + 1] = done[upper, right]
                elif image == 1 and upper == 1 and g > 0:
                    R[1, 0, g - 1] = done[upper, right]
                else:
                    A[image, upper, g] = done[upper, right]
        back = []
        for right in range(2):
            g = 2 * j + right
            s = 6 * image + g
            if image == 0:
                dst, to = (R.at[0, 0, g + 1], near(1, 0)) if g < 5 else (R.at[0, 0, 0], near(1, 1))
                back.append(send(A.at[0, 1, g], dst, r_send.at[s], r_recv.at[s], to))
                if g == 5:
                    back.append(send(A.at[0, 0, 5], R.at[0, 1, 0], r_send.at[12], r_recv.at[12], near(0, 1)))
            else:
                dst, to = (R.at[1, 1, g - 1], near(-1, 0)) if g > 0 else (R.at[1, 1, 5], near(-1, -1))
                back.append(send(A.at[1, 0, g], dst, r_send.at[s], r_recv.at[s], to))
                if g == 0:
                    back.append(send(A.at[1, 1, 0], R.at[1, 0, 5], r_send.at[13], r_recv.at[13], near(0, -1)))
        return back

    crossed = finish(1, final, crossed)
    for copy in crossed:
        copy.wait_recv()
    natural(GP, WP, 128)
    natural(G1, W1, 512)

    def second_rows(n, carry):
        c, x = n // 4, n % 4
        for high in range(2):
            for y in range(4):
                to = pl.multiple_of((x * 32 + high * 16 + c * 8 + y * 2) * 16, 32)
                W2[pl.ds(to, 32)] = G2[c, x, y, 2 * high : 2 * high + 2].reshape(32, 512)
        return carry

    lax.fori_loop(0, 8, second_rows, 0)

    back = {0: [], 1: []}
    for image, j in ((0, 2), (0, 0), (0, 1), (1, 0), (1, 1), (1, 2)):
        back[image] += attend(image, j)

    def mlp(image, half):
        after = T[image, half].reshape(384, 512).astype(F32)
        after = after + layer_norm(R[image, half].reshape(384, 512).astype(F32), gain1_ref[...])
        after = after.astype(BF)
        total = jnp.zeros((384, 512), F32)
        for part in range(4):
            hidden = jnp.dot(after, W1[:, 512 * part : 512 * part + 512], preferred_element_type=F32)
            hidden = 0.5 * hidden * (1.0 + lax.erf(hidden * math.sqrt(0.5)))
            total += jnp.dot(hidden.astype(BF), W2[512 * part : 512 * part + 512], preferred_element_type=F32)
        result = after.astype(F32) + layer_norm(total, gain2_ref[...])
        O[image, half] = result.astype(BF).reshape(6, 64, 512)
        copy = pltpu.make_async_copy(O.at[image, half], out_hbm.at[image, half], out_sem.at[image, half])
        copy.start()
        return copy

    outs = []
    for image in range(2):
        for copy in back[image]:
            copy.wait_recv()
        for half in (1 - image, image):
            outs.append(mlp(image, half))
    for copy in sends:
        copy.wait_send()
    for copy in outs:
        copy.wait()


def body(
    tokens, region, w_qkv, w_proj, w_fc1, w_fc2, gain_attn, gain_mlp, table, index, logit_scale
):
    vmem = pl.BlockSpec(memory_space=pltpu.VMEM)
    DMA = pltpu.SemaphoreType.DMA
    V = pltpu.VMEM
    tiles = (2, 2, 6, 64, 512)
    out = pl.pallas_call(
        kernel,
        out_shape=jax.ShapeDtypeStruct(tiles, BF),
        in_specs=[pl.BlockSpec(memory_space=pl.ANY)] + [vmem] * 9 + [pl.BlockSpec(memory_space=pltpu.SMEM)],
        out_specs=pl.BlockSpec(memory_space=pl.ANY),
        scratch_shapes=[
            V((2, 16, 48, 512), BF), V(tiles, BF), V(tiles, BF), V(tiles, BF), V(tiles, BF), V(tiles, BF),
            V((3, 2, 4, 4, 4, 16, 128), BF), V((2, 4, 4, 4, 16, 128), BF),
            V((2, 4, 4, 4, 16, 512), BF), V((2, 4, 4, 4, 16, 512), BF),
            V((3, 512, 512), BF), V((512, 512), BF), V((512, 2048), BF), V((2048, 512), BF),
            V((6, 3, 4, 256, 128), BF), V((4, 256, 128), BF), V((16, 256, 256), F32), V((8, 16, 128), F32),
            V((3, 16, 128), jnp.int32), V((3, 128, 16), F32), V((256, 128), F32),
            V((4, 256, 128), BF), V((4, 256, 128), BF), V((16, 512), F32),
            DMA((2,)), DMA((2, 2)), DMA((2, 3, 3, 3)), DMA((2, 3, 3, 3)), DMA((2, 3, 4)), DMA((2, 3, 4)),
            DMA((8,)), DMA((8,)), DMA((14,)), DMA((14,)),
        ],
        compiler_params=pltpu.CompilerParams(
            collective_id=0, has_side_effects=True, vmem_limit_bytes=60 * 1024 * 1024
        ),
    )(
        tokens, region, w_qkv, w_proj, w_fc1, w_fc2,
        gain_attn.reshape(1, 512), gain_mlp.reshape(1, 512), table, index, logit_scale,
    )
    out = out.reshape(2, 2, 6, 8, 8, 512).transpose(0, 1, 3, 2, 4, 5)
    return out.reshape(2, 16, 48, 512)


def solution(mesh):
    split = P(("row", "col"), None)
    return jax.shard_map(
        body,
        mesh=mesh,
        in_specs=(P(None, "row", "col", None), P("row", "col"), split, split, split, split, P(), P(), P(), P(), P()),
        out_specs=P(None, "row", "col", None),
        check_vma=False,
    )
```

```python
import math

import jax
import jax.numpy as jnp
from jax import lax
from jax.experimental import pallas as pl
from jax.experimental.pallas import tpu as pltpu
from jax.sharding import PartitionSpec as P

MESH = pl.DeviceIdType.MESH
BF = jnp.bfloat16
F32 = jnp.float32
LOG2E = math.log2(math.e)
ROUTES = ((1, 2, 0), (2, 0, 1), (0, 1, 2))


def iota(shape, dim):
    return lax.broadcasted_iota(jnp.int32, shape, dim)


def layer_norm(value, gain):
    mean = jnp.mean(value, -1, keepdims=True)
    centered = value - mean
    variance = jnp.mean(centered * centered, -1, keepdims=True)
    return centered * lax.rsqrt(variance + 1e-05) * gain


def own_block(w_ref, lo, lanes, tmp):
    for quarter in range(4):
        at = lo + quarter * lanes
        tmp[4 * quarter : 4 * quarter + 4, :lanes] = w_ref[:, at : at + lanes].astype(F32)
    return tmp[:, :lanes].astype(BF)


def kernel(
    tok_hbm, region_ref, wqkv_ref, wproj_ref, wfc1_ref, wfc2_ref,
    gain1_ref, gain2_ref, table_ref, index_ref, scale_ref,
    out_hbm,
    raw, T, X, A, R, O, GQ, GP, G1, G2, WQ, WP, W1, W2,
    QKV, M, bias, tab, RS, RT, LB, FQ, FK, tmp,
    raw_sem, out_sem, p_send, p_recv, g_send, g_recv, d_send, d_recv, h_send, h_recv, r_send, r_recv,
):
    row, col = lax.axis_index("row"), lax.axis_index("col")
    core = lax.rem(row, 2)
    at = (row // 4, col // 2, lax.rem(row // 2, 2) * 2 + lax.rem(col, 2))

    def chip(x, y, z, c):
        return {"row": x * 4 + (z // 2) * 2 + c, "col": y * 2 + lax.rem(z, 2)}

    def near(dr, dc):
        return {"row": lax.rem(row + dr + 16, 16), "col": lax.rem(col + dc + 8, 8)}

    def along(axis, step):
        spot = list(at)
        spot[axis] = lax.rem(spot[axis] + step, 4)
        return chip(*spot, core)

    sibling = chip(*at, 1 - core)
    loads = [pltpu.make_async_copy(tok_hbm.at[i], raw.at[i], raw_sem.at[i]) for i in range(2)]
    for copy in loads:
        copy.start()

    def moved(steps):
        return chip(*[lax.rem(at[a] + steps[a], 4) for a in range(3)], core)

    def plane(route):
        steps = []
        for n in (1, 3, 4, 12, 2, 8, 5, 7, 13, 15, 6, 14, 9, 11, 10):
            step = [0, 0, 0]
            step[route[0]], step[route[1]] = n % 4, n // 4
            steps.append(tuple(step))
        return steps

    steps = sorted({step for route in ROUTES for step in plane(route)})
    peers = [moved(step) for step in steps] + [sibling]
    peers += [near(-1, 0), near(1, 0), near(0, -1), near(0, 1), near(-1, -1), near(1, 1)]
    barrier = pltpu.get_barrier_semaphore()
    for peer in peers:
        pl.semaphore_signal(barrier, inc=1, device_id=peer, device_id_type=MESH)

    for flow in range(3):
        GQ[flow, core, at[0], at[1], at[2]] = own_block(wqkv_ref, 512 * flow, 128, tmp)
    GP[core, at[0], at[1], at[2]] = own_block(wproj_ref, 0, 128, tmp)
    G1[core, at[0], at[1], at[2]] = own_block(wfc1_ref, 0, 512, tmp)
    G2[core, at[0], at[1], at[2]] = wfc2_ref[...]
    RS[0] = jnp.zeros((16, 128), jnp.int32)
    RS[0, :, 0:48] = region_ref[...]

    pl.semaphore_wait(barrier, len(peers))

    sends = []

    def send(src, dst, s_sem, r_sem, device):
        copy = pltpu.make_async_remote_copy(
            src_ref=src, dst_ref=dst, send_sem=s_sem, recv_sem=r_sem,
            device_id=device, device_id_type=MESH,
        )
        copy.start()
        sends.append(copy)
        return copy

    batches = ([GQ.at[0], GQ.at[1], GQ.at[2]], [G1, G2, GP])

    def slab(batch, flow, known, axis=None, step=0):
        spot = list(at)
        if axis is not None:
            spot[axis] = lax.rem(spot[axis] + step, 4)
        pick = tuple(slice(None) if a in known else spot[a] for a in range(3))
        return batches[batch][flow].at[(core,) + pick]

    def spread(batch):
        copies = [[] for flow in range(3)]
        for n in range(15):
            for flow in range(3):
                part = slab(batch, flow, ())
                copies[flow].append(
                    send(part, part, p_send.at[batch, flow, n], p_recv.at[batch, flow, n], moved(plane(ROUTES[flow])[n]))
                )
        return copies

    def lines(batch, flow):
        route = ROUTES[flow]
        part = slab(batch, flow, route[:2])
        return [
            send(part, part, g_send.at[batch, flow, t - 1], g_recv.at[batch, flow, t - 1], along(route[2], t))
            for t in (1, 3, 2)
        ]

    def across(batch, flow, piece):
        route = ROUTES[flow]
        part = slab(batch, flow, route[:2], route[2], piece)
        return send(part, part, d_send.at[batch, flow, piece], d_recv.at[batch, flow, piece], sibling)

    def last_step(batch, flows, planes):
        final, crossed = {}, []
        for flow in flows:
            for copy in planes[flow]:
                copy.wait_recv()
            final[flow] = lines(batch, flow)
        for flow in flows:
            crossed.append(across(batch, flow, 0))
        return final, crossed

    def pass_on(batch, final, crossed, orders=(0, 1, 2)):
        for order in orders:
            for flow in final:
                final[flow][order].wait_recv()
                crossed.append(across(batch, flow, (3, 1, 2)[order]))

    first = spread(0)

    halo = [
        send(RS.at[0], RS.at[1], h_send.at[6], h_recv.at[6], near(1, 0)),
        send(RS.at[0], RS.at[2], h_send.at[7], h_recv.at[7], near(1, 1)),
    ]
    for image in range(2):
        loads[image].wait()
        for half in (image, 1 - image):
            rows = raw[image, 8 * half : 8 * half + 8].astype(F32)
            for group in range(6):
                part = rows[:, 8 * group : 8 * group + 8, :].reshape(64, 512).astype(BF)
                T[image, half, group] = part
                if image == 0 and half == 1 and group > 0:
                    X[0, 0, group - 1] = part
                if image == 1 and half == 0 and group < 5:
                    X[1, 1, group + 1] = part
        if image == 0:
            halo.append(send(T.at[0, 0, 1:6], X.at[0, 1, 0:5], h_send.at[0], h_recv.at[0], near(-1, 0)))
            halo.append(send(T.at[0, 0, 0], X.at[0, 1, 5], h_send.at[1], h_recv.at[1], near(-1, -1)))
            halo.append(send(T.at[0, 1, 0], X.at[0, 0, 5], h_send.at[2], h_recv.at[2], near(0, -1)))
        else:
            halo.append(send(T.at[1, 1, 0:5], X.at[1, 0, 1:6], h_send.at[3], h_recv.at[3], near(1, 0)))
            halo.append(send(T.at[1, 1, 5], X.at[1, 0, 0], h_send.at[4], h_recv.at[4], near(1, 1)))
            halo.append(send(T.at[1, 0, 5], X.at[1, 1, 0], h_send.at[5], h_recv.at[5], near(0, 1)))


    levels = jnp.round((2048.0 * 16.0 * LOG2E) * jax.nn.sigmoid(table_ref[...])).astype(jnp.int32)
    pairs = levels[0:8] + (levels[8:16] - 32768) * 65536
    for chunk in range(7):
        tab[chunk] = pairs[:, 128 * chunk : 128 * chunk + 128]
    tab[7, :, 0:65] = pairs[:, 896:961]
    lane = iota((8, 128), 1)
    reorder = (lane // 8 % 8) * 16 + (lane // 64) * 8 + lane % 8

    def bias_rows(start, stop):
        def one(n, carry):
            source = (n // 16) * 128 + (n % 8) * 16 + (n // 8 % 2) * 8
            to = pl.ds(pl.multiple_of(n * 8, 8), 8)
            for half in range(2):
                lanes = slice(128 * half, 128 * half + 128)
                index = index_ref[pl.ds(pl.multiple_of(source, 8), 8), lanes]
                index = jnp.take_along_axis(index, reorder, axis=1, mode="promise_in_bounds")
                high, low = index // 128, index % 128
                for head in range(8):
                    found = jnp.zeros((8, 128), jnp.int32)
                    for chunk in range(8):
                        entry = jnp.broadcast_to(tab[chunk, head : head + 1, :], (8, 128))
                        value = jnp.take_along_axis(entry, low, axis=1, mode="promise_in_bounds")
                        found = jnp.where(high == chunk, value, found)
                    bias[head, to, lanes] = (found & 65535).astype(F32) * (1.0 / 2048.0)
                    bias[head + 8, to, lanes] = (found >> 16).astype(F32) * (1.0 / 2048.0) + 16.0
            return carry

        lax.fori_loop(start, stop, one, 0)

    bias_rows(0, 6)
    final, crossed = last_step(0, (0, 1, 2), first)
    other = spread(1)
    bias_rows(6, 24)
    pass_on(0, final, crossed)
    bias_rows(24, 32)

    for copy in halo[:2]:
        copy.wait_recv()
    for place in range(3):
        RT[place] = RS[place].astype(F32).T

    o, i = iota((256, 256), 0), iota((256, 256), 1)
    spot = (o // 8 % 4) * 64 + (o // 32 % 2) * 32 + (o // 4 % 2) * 16 + (o // 64) * 4 + o % 4
    permute = jnp.where(spot == i, 1.0, 0.0).astype(BF)
    squares = jnp.where(o // 32 == i // 32, 1.0, 0.0).astype(BF)

    def natural(sources, dests, lanes, unroll):
        def one(n, carry):
            c, x = n // 4, n % 4
            block = jnp.concatenate([source[c, x].reshape(256, lanes) for source in sources], 1)
            found = jnp.dot(permute, block, preferred_element_type=F32).astype(BF)
            for k, dest in enumerate(dests):
                for quarter in range(4):
                    for high in range(2):
                        base = 64 * quarter + 32 * high
                        to = pl.multiple_of(x * 128 + high * 64 + c * 32, 32)
                        dest[pl.ds(to, 32), lanes * quarter : lanes * quarter + lanes] = found[
                            base : base + 32, lanes * k : lanes * k + lanes
                        ]
            return carry

        lax.fori_loop(0, 8, one, 0, unroll=unroll)

    for copy in crossed:
        copy.wait_recv()
    natural([GQ.at[flow] for flow in range(3)], [WQ.at[flow] for flow in range(3)], 128, True)

    lane512 = iota((1, 512), 1)
    scale = jnp.zeros((1, 512), F32)
    for head in range(16):
        scale = jnp.where(lane512 // 32 == head, scale_ref[head] * LOG2E, scale)

    def project(image, upper):
        x = X[image, upper].reshape(384, 512)
        for kind in range(3):
            value = jnp.dot(x, WQ[kind], preferred_element_type=F32)
            if kind < 2:
                square = (value * value).astype(BF)
                length = jnp.concatenate(
                    [jnp.dot(square[:, 256 * s : 256 * s + 256], squares, preferred_element_type=F32) for s in range(2)], 1)
                unit = lax.rsqrt(jnp.maximum(length, 1.0))
                value = value * (unit * scale if kind == 0 else unit)
            value = value.astype(BF)
            for j in range(3):
                for block in range(4):
                    QKV[3 * image + j, kind, block, 128 * upper : 128 * upper + 128] = value[
                        128 * j : 128 * j + 128, 128 * block : 128 * block + 128
                    ]

    side = {0: halo[4], 1: halo[7]}
    for image in range(2):
        side[image].wait_recv()
        project(image, image)
    final, crossed = last_step(1, (2, 0, 1), other)
    for image in range(2):
        for copy in halo[2 + 3 * image : 4 + 3 * image]:
            copy.wait_recv()
        project(image, 1 - image)

    lane128 = iota((1, 128), 1)
    ones = jnp.ones((256, 128), BF)

    def attend(image, j):
        w = 3 * image + j
        place, start = (0, 16 * j) if image == 0 else ((2, 32) if j == 0 else (1, 16 * (j - 1)))
        for n in range(32):
            a, b = (n // 16) * 8 + n % 8, n // 8 % 2
            LB[8 * n : 8 * n + 8] = jnp.broadcast_to(RT[place, start + 8 * b : start + 8 * b + 8, a : a + 1], (8, 128))
        label = LB[...]
        for i in range(4):
            m = lane128 - 32 * ((i + 1) % 4)
            target = jnp.where((m >= 0) & (m < 6), m % 3, -1).astype(F32)
            hi, lo = 144.0, 100.0 * LOG2E - 144.0
            big = jnp.where(m < 3, hi, lo)
            rest = jnp.where(m == 6, -hi, jnp.where(m == 7, -lo, 0.0))
            unit = jnp.where((m == 6) | (m == 7), 1.0, 0.0)
            same = label == target
            FQ[i] = jnp.where(same, big, rest).astype(BF)
            FK[i] = jnp.where(same, 1.0, unit).astype(BF)

        def heads(block, carry):
            q, k = QKV[w, 0, block], QKV[w, 1, block]
            v = jnp.concatenate([QKV[w, 2, block], ones], 1)
            top = jnp.zeros((256, 128), F32)
            total = jnp.zeros((256, 128), F32)
            for i in range(4):
                here = lane128 // 32 == i
                keep = jnp.where(here, 1.0, 0.0).astype(BF)
                qh = q * keep + FQ[i]
                kh = k * keep + FK[i]
                score = lax.dot_general(qh, kh, (((1,), (1,)), ((), ())), preferred_element_type=F32)
                weight = jnp.exp2(score + bias[4 * block + i]).astype(BF)
                found = jnp.dot(weight, v, preferred_element_type=F32)
                top = jnp.where(here, found[:, :128], top)
                total = jnp.where(here, found[:, 128:], total)
            M[block] = (top / total).astype(BF)
            return carry

        lax.fori_loop(0, 4, heads, 0)
        mixed = jnp.concatenate([M[b] for b in range(4)], 1)
        done = jnp.dot(mixed, WP[...], preferred_element_type=F32).astype(BF).reshape(2, 2, 64, 512)
        for upper in range(2):
            for right in range(2):
                g = 2 * j + right
                if image == 0 and upper == 0 and g < 5:
                    R[0, 1, g + 1] = done[upper, right]
                elif image == 1 and upper == 1 and g > 0:
                    R[1, 0, g - 1] = done[upper, right]
                else:
                    A[image, upper, g] = done[upper, right]
        back = []
        for right in range(2):
            g = 2 * j + right
            s = 6 * image + g
            if image == 0:
                dst, to = (R.at[0, 0, g + 1], near(1, 0)) if g < 5 else (R.at[0, 0, 0], near(1, 1))
                back.append(send(A.at[0, 1, g], dst, r_send.at[s], r_recv.at[s], to))
                if g == 5:
                    back.append(send(A.at[0, 0, 5], R.at[0, 1, 0], r_send.at[12], r_recv.at[12], near(0, 1)))
            else:
                dst, to = (R.at[1, 1, g - 1], near(-1, 0)) if g > 0 else (R.at[1, 1, 5], near(-1, -1))
                back.append(send(A.at[1, 0, g], dst, r_send.at[s], r_recv.at[s], to))
                if g == 0:
                    back.append(send(A.at[1, 1, 0], R.at[1, 0, 5], r_send.at[13], r_recv.at[13], near(0, -1)))
        return back

    def second_rows(n, carry):
        c, x = n // 4, n % 4
        for high in range(2):
            for y in range(4):
                to = pl.multiple_of((x * 32 + high * 16 + c * 8 + y * 2) * 16, 32)
                W2[pl.ds(to, 32)] = G2[c, x, y, 2 * high : 2 * high + 2].reshape(32, 512)
        return carry

    back = {0: [], 1: []}
    ready = {2: final.pop(2)}
    proj = [crossed.pop(0)]
    pass_on(1, ready, proj)
    for copy in proj:
        copy.wait_recv()
    natural([GP], [WP], 128, 2)
    for n, (image, j) in enumerate(((0, 2), (0, 0), (0, 1), (1, 0), (1, 1), (1, 2))):
        back[image] += attend(image, j)
        if n in (0, 1, 2):
            pass_on(1, final, crossed, (n,))
    for copy in crossed:
        copy.wait_recv()
    natural([G1], [W1], 512, 2)
    lax.fori_loop(0, 8, second_rows, 0)

    def mlp(image, half):
        after = T[image, half].reshape(384, 512).astype(F32)
        after = after + layer_norm(R[image, half].reshape(384, 512).astype(F32), gain1_ref[...])
        after = after.astype(BF)
        total = jnp.zeros((384, 512), F32)
        for part in range(4):
            hidden = jnp.dot(after, W1[:, 512 * part : 512 * part + 512], preferred_element_type=F32)
            hidden = 0.5 * hidden * (1.0 + lax.erf(hidden * math.sqrt(0.5)))
            total += jnp.dot(hidden.astype(BF), W2[512 * part : 512 * part + 512], preferred_element_type=F32)
        result = after.astype(F32) + layer_norm(total, gain2_ref[...])
        result = result.reshape(6, 8, 8, 512)
        O[image, half] = jnp.concatenate([result[g] for g in range(6)], 1).astype(BF)
        copy = pltpu.make_async_copy(O.at[image, half], out_hbm.at[image, 8 * half : 8 * half + 8], out_sem.at[image, half])
        copy.start()
        return copy

    outs = []
    for image in range(2):
        for copy in back[image]:
            copy.wait_recv()
        for half in (1 - image, image):
            outs.append(mlp(image, half))
    for copy in sends:
        copy.wait_send()
    for copy in outs:
        copy.wait()


def body(
    tokens, region, w_qkv, w_proj, w_fc1, w_fc2, gain_attn, gain_mlp, table, index, logit_scale
):
    vmem = pl.BlockSpec(memory_space=pltpu.VMEM)
    DMA = pltpu.SemaphoreType.DMA
    V = pltpu.VMEM
    tiles = (2, 2, 6, 64, 512)
    return pl.pallas_call(
        kernel,
        out_shape=jax.ShapeDtypeStruct((2, 16, 48, 512), BF),
        in_specs=[pl.BlockSpec(memory_space=pl.ANY)] + [vmem] * 9 + [pl.BlockSpec(memory_space=pltpu.SMEM)],
        out_specs=pl.BlockSpec(memory_space=pl.ANY),
        scratch_shapes=[
            V((2, 16, 48, 512), BF), V(tiles, BF), V(tiles, BF), V(tiles, BF), V(tiles, BF), V((2, 2, 8, 48, 512), BF),
            V((3, 2, 4, 4, 4, 16, 128), BF), V((2, 4, 4, 4, 16, 128), BF),
            V((2, 4, 4, 4, 16, 512), BF), V((2, 4, 4, 4, 16, 512), BF),
            V((3, 512, 512), BF), V((512, 512), BF), V((512, 2048), BF), V((2048, 512), BF),
            V((6, 3, 4, 256, 128), BF), V((4, 256, 128), BF), V((16, 256, 256), F32), V((8, 8, 128), jnp.int32),
            V((3, 16, 128), jnp.int32), V((3, 128, 16), F32), V((256, 128), F32),
            V((4, 256, 128), BF), V((4, 256, 128), BF), V((16, 512), F32),
            DMA((2,)), DMA((2, 2)), DMA((2, 3, 15)), DMA((2, 3, 15)), DMA((2, 3, 3)), DMA((2, 3, 3)), DMA((2, 3, 4)), DMA((2, 3, 4)),
            DMA((8,)), DMA((8,)), DMA((14,)), DMA((14,)),
        ],
        compiler_params=pltpu.CompilerParams(
            collective_id=0, has_side_effects=True, vmem_limit_bytes=60 * 1024 * 1024
        ),
    )(
        tokens, region, w_qkv, w_proj, w_fc1, w_fc2,
        gain_attn.reshape(1, 512), gain_mlp.reshape(1, 512), table.T, index, logit_scale,
    )


def solution(mesh):
    split = P(("row", "col"), None)
    return jax.shard_map(
        body,
        mesh=mesh,
        in_specs=(P(None, "row", "col", None), P("row", "col"), split, split, split, split, P(), P(), P(), P(), P()),
        out_specs=P(None, "row", "col", None),
        check_vma=False,
    )
```

```python
import math

import jax
import jax.numpy as jnp
from jax import lax
from jax.experimental import pallas as pl
from jax.experimental.pallas import tpu as pltpu
from jax.sharding import PartitionSpec as P

MESH = pl.DeviceIdType.MESH
BF = jnp.bfloat16
F32 = jnp.float32
LOG2E = math.log2(math.e)
ROUTES = ((1, 0), (0, 1))


def iota(shape, dim):
    return lax.broadcasted_iota(jnp.int32, shape, dim)


def layer_norm(value, gain):
    mean = jnp.mean(value, -1, keepdims=True)
    centered = value - mean
    variance = jnp.mean(centered * centered, -1, keepdims=True)
    return centered * lax.rsqrt(variance + 1e-05) * gain


def own_block(w_ref, lo, lanes, tmp):
    for quarter in range(4):
        at = lo + quarter * lanes
        tmp[4 * quarter : 4 * quarter + 4, :lanes] = w_ref[:, at : at + lanes].astype(F32)
    return tmp[:, :lanes].astype(BF)


def kernel(
    tok_hbm, region_hbm, wqkv_hbm, wproj_hbm, wfc1_hbm, wfc2_hbm,
    gain1_hbm, gain2_hbm, table_hbm, index_hbm, scale_ref,
    out_hbm,
    region_ref, wqkv_ref, wproj_ref, wfc1_ref, wfc2_ref, gain1_ref, gain2_ref, table_ref, index_ref,
    raw, T, X, A, R, O, GQ, GP, GF, WQ, WP, W1, W2,
    QKV, M, bias, tab, RS, RT, LB, FQ, FK, tmp,
    raw_sem, in_sem, out_sem, z_send, z_recv, g_send, g_recv, d_send, d_recv, h_send, h_recv, r_send, r_recv,
):
    row, col = lax.axis_index("row"), lax.axis_index("col")
    core = row & 1
    at = (row >> 2, col >> 1, (row & 2) + (col & 1))

    def chip(x, y, z, c):
        return {"row": x * 4 + (z & 2) + c, "col": y * 2 + (z & 1)}

    def near(dr, dc):
        return {"row": (row + dr + 16) & 15, "col": (col + dc + 8) & 7}

    def along(axis, step):
        spot = list(at)
        spot[axis] = (spot[axis] + step) & 3
        return chip(*spot, core)

    sibling = chip(*at, 1 - core)
    peers = [along(axis, step) for axis in range(3) for step in (1, 2, 3)] + [sibling]
    peers += [near(-1, 0), near(1, 0), near(0, -1), near(0, 1), near(-1, -1), near(1, 1)]
    barrier = pltpu.get_barrier_semaphore()
    for peer in peers:
        pl.semaphore_signal(barrier, inc=1, device_id=peer, device_id_type=MESH)

    inputs = [
        pltpu.make_async_copy(source, dest, in_sem.at[n])
        for n, (source, dest) in enumerate((
            (wqkv_hbm, wqkv_ref), (wproj_hbm, wproj_ref), (region_hbm, region_ref), (wfc1_hbm, wfc1_ref),
            (wfc2_hbm, wfc2_ref), (table_hbm, table_ref), (index_hbm, index_ref), (gain1_hbm, gain1_ref), (gain2_hbm, gain2_ref),
        ))
    ]
    loads = [pltpu.make_async_copy(tok_hbm.at[i], raw.at[i], raw_sem.at[i]) for i in range(2)]
    for copy in inputs + loads:
        copy.start()
    for copy in inputs:
        copy.wait()

    here = (core, at[0], at[1], at[2])
    for flow in range(3):
        GQ[here + (slice(None), slice(128 * flow, 128 * flow + 128))] = own_block(wqkv_ref, 512 * flow, 128, tmp)
    GP[here] = own_block(wproj_ref, 0, 128, tmp)
    GF[here + (slice(None), slice(0, 512))] = own_block(wfc1_ref, 0, 512, tmp)
    GF[here + (slice(None), slice(512, 1024))] = wfc2_ref[...]
    RS[0] = jnp.zeros((16, 128), jnp.int32)
    RS[0, :, 0:48] = region_ref[...]

    for image in range(2):
        loads[image].wait()
        for half in (image, 1 - image):
            rows = raw[image, 8 * half : 8 * half + 8].astype(F32)
            for group in range(6):
                part = rows[:, 8 * group : 8 * group + 8, :].reshape(64, 512).astype(BF)
                T[image, half, group] = part
                if image == 0 and half == 1 and group > 0:
                    X[0, 0, group - 1] = part
                if image == 1 and half == 0 and group < 5:
                    X[1, 1, group + 1] = part

    pl.semaphore_wait(barrier, len(peers))

    sends = []

    def send(src, dst, s_sem, r_sem, device):
        copy = pltpu.make_async_remote_copy(
            src_ref=src, dst_ref=dst, send_sem=s_sem, recv_sem=r_sem,
            device_id=device, device_id_type=MESH,
        )
        copy.start()
        sends.append(copy)
        return copy

    batches = (GQ, GP, GF)

    def step_z(batch):
        part = batches[batch].at[here]
        return [send(part, part, z_send.at[batch, t - 1], z_recv.at[batch, t - 1], along(2, t)) for t in (1, 3, 2)]

    def slab(batch, flow, step, shift=0):
        spot = list(at[:2])
        axis = ROUTES[flow][step]
        spot[axis] = (spot[axis] + shift) & 3
        if step == 1:
            spot[ROUTES[flow][0]] = slice(None)
        return batches[batch].at[core, spot[0], spot[1], 2 * flow : 2 * flow + 2]

    def step_xy(batch, step, before):
        copies = {}
        if step == 0:
            for copy in before:
                copy.wait_recv()
        for flow in range(2):
            if step == 1:
                for copy in before[flow]:
                    copy.wait_recv()
            part = slab(batch, flow, step)
            copies[flow] = [
                send(part, part, g_send.at[batch, flow, step, t - 1], g_recv.at[batch, flow, step, t - 1],
                     along(ROUTES[flow][step], t))
                for t in (1, 3, 2)
            ]
        return copies

    def across(batch, flow, piece):
        part = slab(batch, flow, 1, piece)
        return send(part, part, d_send.at[batch, flow, piece], d_recv.at[batch, flow, piece], sibling)

    def pass_on(batch, final, orders=(0, 1, 2)):
        crossed = []
        for order in orders:
            for flow in range(2):
                final[flow][order].wait_recv()
                crossed.append(across(batch, flow, (3, 1, 2)[order]))
        return crossed

    qkv = step_z(0)
    halo = [
        send(RS.at[0], RS.at[1], h_send.at[6], h_recv.at[6], near(1, 0)),
        send(RS.at[0], RS.at[2], h_send.at[7], h_recv.at[7], near(1, 1)),
        send(T.at[0, 0, 1:6], X.at[0, 1, 0:5], h_send.at[0], h_recv.at[0], near(-1, 0)),
        send(T.at[0, 0, 0], X.at[0, 1, 5], h_send.at[1], h_recv.at[1], near(-1, -1)),
        send(T.at[0, 1, 0], X.at[0, 0, 5], h_send.at[2], h_recv.at[2], near(0, -1)),
        send(T.at[1, 1, 0:5], X.at[1, 0, 1:6], h_send.at[3], h_recv.at[3], near(1, 0)),
        send(T.at[1, 1, 5], X.at[1, 0, 0], h_send.at[4], h_recv.at[4], near(1, 1)),
        send(T.at[1, 0, 5], X.at[1, 1, 0], h_send.at[5], h_recv.at[5], near(0, 1)),
    ]
    proj = step_z(1)
    fc = step_z(2)

    levels = jnp.round((2048.0 * 16.0 * LOG2E) * jax.nn.sigmoid(table_ref[...])).astype(jnp.int32)
    pairs = levels[0:8] + (levels[8:16] - 32768) * 65536
    for chunk in range(7):
        tab[chunk] = pairs[:, 128 * chunk : 128 * chunk + 128]
    tab[7, :, 0:65] = pairs[:, 896:961]
    lane = iota((8, 128), 1)
    reorder = (lane // 8 % 8) * 16 + (lane // 64) * 8 + lane % 8

    def bias_rows(start, stop):
        def one(n, carry):
            source = (n // 16) * 128 + (n % 8) * 16 + (n // 8 % 2) * 8
            to = pl.ds(pl.multiple_of(n * 8, 8), 8)
            for half in range(2):
                lanes = slice(128 * half, 128 * half + 128)
                index = index_ref[pl.ds(pl.multiple_of(source, 8), 8), lanes]
                index = jnp.take_along_axis(index, reorder, axis=1, mode="promise_in_bounds")
                high, low = index // 128, index % 128
                for head in range(8):
                    found = jnp.zeros((8, 128), jnp.int32)
                    for chunk in range(8):
                        entry = jnp.broadcast_to(tab[chunk, head : head + 1, :], (8, 128))
                        value = jnp.take_along_axis(entry, low, axis=1, mode="promise_in_bounds")
                        found = jnp.where(high == chunk, value, found)
                    bias[head, to, lanes] = (found & 65535).astype(F32) * (1.0 / 2048.0)
                    bias[head + 8, to, lanes] = (found >> 16).astype(F32) * (1.0 / 2048.0) + 16.0
            return carry

        lax.fori_loop(start, stop, one, 0)

    bias_rows(0, 8)
    qkv = step_xy(0, 0, qkv)
    bias_rows(8, 20)
    qkv = step_xy(0, 1, qkv)
    crossed = [across(0, flow, 0) for flow in range(2)]
    proj = step_xy(1, 0, proj)
    bias_rows(20, 32)

    for copy in halo[:2]:
        copy.wait_recv()
    for place in range(3):
        RT[place] = RS[place].astype(F32).T

    o, i = iota((256, 256), 0), iota((256, 256), 1)
    spot = (o // 8 % 4) * 64 + (o // 32 % 2) * 32 + (o // 4 % 2) * 16 + (o // 64) * 4 + o % 4
    permute = jnp.where(spot == i, 1.0, 0.0).astype(BF)
    squares = jnp.where(o // 32 == i // 32, 1.0, 0.0).astype(BF)

    def natural(source, first, lanes, dests, unroll):
        def one(n, carry):
            c, x = n // 4, n % 4
            block = source[c, x, :, :, :, first : first + lanes * len(dests)].reshape(256, lanes * len(dests))
            found = jnp.dot(permute, block, preferred_element_type=F32).astype(BF)
            for k, dest in enumerate(dests):
                for quarter in range(4):
                    for high in range(2):
                        base = 64 * quarter + 32 * high
                        to = pl.multiple_of(x * 128 + high * 64 + c * 32, 32)
                        dest[pl.ds(to, 32), lanes * quarter : lanes * quarter + lanes] = found[
                            base : base + 32, lanes * k : lanes * k + lanes
                        ]
            return carry

        lax.fori_loop(0, 8, one, 0, unroll=unroll)

    crossed += pass_on(0, qkv)
    proj = step_xy(1, 1, proj)
    crossed_proj = [across(1, flow, 0) for flow in range(2)]
    fc = step_xy(2, 0, fc)
    for copy in crossed:
        copy.wait_recv()
    natural(GQ, 0, 128, [WQ.at[flow] for flow in range(3)], True)

    lane512 = iota((1, 512), 1)
    scale = jnp.zeros((1, 512), F32)
    for head in range(16):
        scale = jnp.where(lane512 // 32 == head, scale_ref[head] * LOG2E, scale)

    def project(image, upper):
        x = X[image, upper].reshape(384, 512)
        for kind in range(3):
            value = jnp.dot(x, WQ[kind], preferred_element_type=F32)
            if kind < 2:
                square = (value * value).astype(BF)
                length = jnp.concatenate(
                    [jnp.dot(square[:, 256 * s : 256 * s + 256], squares, preferred_element_type=F32) for s in range(2)], 1)
                unit = lax.rsqrt(jnp.maximum(length, 1.0))
                value = value * (unit * scale if kind == 0 else unit)
            value = value.astype(BF)
            for j in range(3):
                for block in range(4):
                    QKV[3 * image + j, kind, block, 128 * upper : 128 * upper + 128] = value[
                        128 * j : 128 * j + 128, 128 * block : 128 * block + 128
                    ]

    side = {0: halo[4], 1: halo[7]}
    for image in range(2):
        side[image].wait_recv()
        project(image, image)
    crossed_proj += pass_on(1, proj)
    for image in range(2):
        for copy in halo[2 + 3 * image : 4 + 3 * image]:
            copy.wait_recv()
        project(image, 1 - image)
    fc = step_xy(2, 1, fc)
    crossed = [across(2, flow, 0) for flow in range(2)]

    lane128 = iota((1, 128), 1)
    ones = jnp.ones((256, 128), BF)

    def attend(image, j):
        w = 3 * image + j
        place, start = (0, 16 * j) if image == 0 else ((2, 32) if j == 0 else (1, 16 * (j - 1)))
        for n in range(32):
            a, b = (n // 16) * 8 + n % 8, n // 8 % 2
            LB[8 * n : 8 * n + 8] = jnp.broadcast_to(RT[place, start + 8 * b : start + 8 * b + 8, a : a + 1], (8, 128))
        label = LB[...]
        for i in range(4):
            m = lane128 - 32 * ((i + 1) % 4)
            target = jnp.where((m >= 0) & (m < 6), m % 3, -1).astype(F32)
            hi, lo = 144.0, 100.0 * LOG2E - 144.0
            big = jnp.where(m < 3, hi, lo)
            rest = jnp.where(m == 6, -hi, jnp.where(m == 7, -lo, 0.0))
            unit = jnp.where((m == 6) | (m == 7), 1.0, 0.0)
            same = label == target
            FQ[i] = jnp.where(same, big, rest).astype(BF)
            FK[i] = jnp.where(same, 1.0, unit).astype(BF)

        for block in range(4):
            q, k = QKV[w, 0, block], QKV[w, 1, block]
            v = jnp.concatenate([QKV[w, 2, block], ones], 1)
            top = jnp.zeros((256, 128), F32)
            total = jnp.zeros((256, 128), F32)
            for i in range(4):
                here = lane128 // 32 == i
                keep = jnp.where(here, 1.0, 0.0).astype(BF)
                qh = q * keep + FQ[i]
                kh = k * keep + FK[i]
                score = lax.dot_general(qh, kh, (((1,), (1,)), ((), ())), preferred_element_type=F32)
                weight = jnp.exp2(score + bias[4 * block + i]).astype(BF)
                found = jnp.dot(weight, v, preferred_element_type=F32)
                top = jnp.where(here, found[:, :128], top)
                total = jnp.where(here, found[:, 128:], total)
            M[block] = (top / total).astype(BF)
        mixed = jnp.concatenate([M[b] for b in range(4)], 1)
        done = jnp.dot(mixed, WP[...], preferred_element_type=F32).astype(BF).reshape(2, 2, 64, 512)
        for upper in range(2):
            for right in range(2):
                g = 2 * j + right
                if image == 0 and upper == 0 and g < 5:
                    R[0, 1, g + 1] = done[upper, right]
                elif image == 1 and upper == 1 and g > 0:
                    R[1, 0, g - 1] = done[upper, right]
                else:
                    A[image, upper, g] = done[upper, right]
        back = []
        for right in range(2):
            g = 2 * j + right
            s = 6 * image + g
            if image == 0:
                dst, to = (R.at[0, 0, g + 1], near(1, 0)) if g < 5 else (R.at[0, 0, 0], near(1, 1))
                back.append(send(A.at[0, 1, g], dst, r_send.at[s], r_recv.at[s], to))
                if g == 5:
                    back.append(send(A.at[0, 0, 5], R.at[0, 1, 0], r_send.at[12], r_recv.at[12], near(0, 1)))
            else:
                dst, to = (R.at[1, 1, g - 1], near(-1, 0)) if g > 0 else (R.at[1, 1, 5], near(-1, -1))
                back.append(send(A.at[1, 0, g], dst, r_send.at[s], r_recv.at[s], to))
                if g == 0:
                    back.append(send(A.at[1, 1, 0], R.at[1, 0, 5], r_send.at[13], r_recv.at[13], near(0, -1)))
        return back

    def second_rows(n, carry):
        c, x = n // 4, n % 4
        for high in range(2):
            for y in range(4):
                to = pl.multiple_of((x * 32 + high * 16 + c * 8 + y * 2) * 16, 32)
                W2[pl.ds(to, 32)] = GF[c, x, y, 2 * high : 2 * high + 2, :, 512:1024].reshape(32, 512)
        return carry

    back = {0: [], 1: []}
    for copy in crossed_proj:
        copy.wait_recv()
    natural(GP, 0, 128, [WP], True)
    for n, (image, j) in enumerate(((0, 2), (0, 0), (0, 1), (1, 0), (1, 1), (1, 2))):
        back[image] += attend(image, j)
        if n >= 3:
            crossed += pass_on(2, fc, (n - 3,))
    for copy in crossed:
        copy.wait_recv()
    natural(GF, 0, 512, [W1], 4)
    lax.fori_loop(0, 8, second_rows, 0)

    def mlp(image, half):
        after = T[image, half].reshape(384, 512).astype(F32)
        after = after + layer_norm(R[image, half].reshape(384, 512).astype(F32), gain1_ref[...])
        after = after.astype(BF)
        total = jnp.zeros((384, 512), F32)
        for part in range(4):
            hidden = jnp.dot(after, W1[:, 512 * part : 512 * part + 512], preferred_element_type=F32)
            hidden = 0.5 * hidden * (1.0 + lax.erf(hidden * math.sqrt(0.5)))
            total += jnp.dot(hidden.astype(BF), W2[512 * part : 512 * part + 512], preferred_element_type=F32)
        result = after.astype(F32) + layer_norm(total, gain2_ref[...])
        result = result.reshape(6, 8, 8, 512)
        O[image, half] = jnp.concatenate([result[g] for g in range(6)], 1).astype(BF)
        copy = pltpu.make_async_copy(O.at[image, half], out_hbm.at[image, 8 * half : 8 * half + 8], out_sem.at[image, half])
        copy.start()
        return copy

    outs = []
    for image in range(2):
        for copy in back[image]:
            copy.wait_recv()
        for half in (1 - image, image):
            outs.append(mlp(image, half))
    for copy in sends:
        copy.wait_send()
    for copy in outs:
        copy.wait()


def body(
    tokens, region, w_qkv, w_proj, w_fc1, w_fc2, gain_attn, gain_mlp, table, index, logit_scale
):
    DMA = pltpu.SemaphoreType.DMA
    V = pltpu.VMEM
    tiles = (2, 2, 6, 64, 512)
    return pl.pallas_call(
        kernel,
        out_shape=jax.ShapeDtypeStruct((2, 16, 48, 512), BF),
        in_specs=[pl.BlockSpec(memory_space=pl.ANY)] * 10 + [pl.BlockSpec(memory_space=pltpu.SMEM)],
        out_specs=pl.BlockSpec(memory_space=pl.ANY),
        scratch_shapes=[
            V((16, 48), jnp.int32), V((4, 1536), BF), V((4, 512), BF), V((4, 2048), BF), V((16, 512), BF),
            V((1, 512), F32), V((1, 512), F32), V((16, 961), F32), V((256, 256), jnp.int32),
            V((2, 16, 48, 512), BF), V(tiles, BF), V(tiles, BF), V(tiles, BF), V(tiles, BF), V((2, 2, 8, 48, 512), BF),
            V((2, 4, 4, 4, 16, 384), BF), V((2, 4, 4, 4, 16, 128), BF), V((2, 4, 4, 4, 16, 1024), BF),
            V((3, 512, 512), BF), V((512, 512), BF), V((512, 2048), BF), V((2048, 512), BF),
            V((6, 3, 4, 256, 128), BF), V((4, 256, 128), BF), V((16, 256, 256), F32), V((8, 8, 128), jnp.int32),
            V((3, 16, 128), jnp.int32), V((3, 128, 16), F32), V((256, 128), F32),
            V((4, 256, 128), BF), V((4, 256, 128), BF), V((16, 512), F32),
            DMA((2,)), DMA((9,)), DMA((2, 2)), DMA((3, 3)), DMA((3, 3)), DMA((3, 2, 2, 3)), DMA((3, 2, 2, 3)), DMA((3, 2, 4)), DMA((3, 2, 4)),
            DMA((8,)), DMA((8,)), DMA((14,)), DMA((14,)),
        ],
        compiler_params=pltpu.CompilerParams(
            collective_id=0, has_side_effects=True, vmem_limit_bytes=60 * 1024 * 1024
        ),
    )(
        tokens, region, w_qkv, w_proj, w_fc1, w_fc2,
        gain_attn.reshape(1, 512), gain_mlp.reshape(1, 512), table.T, index, logit_scale,
    )


def solution(mesh):
    split = P(("row", "col"), None)
    return jax.shard_map(
        body,
        mesh=mesh,
        in_specs=(P(None, "row", "col", None), P("row", "col"), split, split, split, split, P(), P(), P(), P(), P()),
        out_specs=P(None, "row", "col", None),
        check_vma=False,
    )
```

```python
import math

import jax
import jax.numpy as jnp
from jax import lax
from jax.experimental import pallas as pl
from jax.experimental.pallas import tpu as pltpu
from jax.sharding import PartitionSpec as P

MESH = pl.DeviceIdType.MESH
BF = jnp.bfloat16
F32 = jnp.float32
LOG2E = math.log2(math.e)
ROUTES = ((1, 0), (0, 1))


def iota(shape, dim):
    return lax.broadcasted_iota(jnp.int32, shape, dim)


def layer_norm(value, gain):
    mean = jnp.mean(value, -1, keepdims=True)
    centered = value - mean
    variance = jnp.mean(centered * centered, -1, keepdims=True)
    return centered * lax.rsqrt(variance + 1e-05) * gain


def own_block(w_ref, lo, lanes, tmp):
    for quarter in range(4):
        at = lo + quarter * lanes
        tmp[4 * quarter : 4 * quarter + 4, :lanes] = w_ref[:, at : at + lanes].astype(F32)
    return tmp[:, :lanes].astype(BF)


def kernel(
    tok_hbm, region_hbm, wqkv_hbm, wproj_hbm, wfc1_hbm, wfc2_hbm,
    gain1_hbm, gain2_hbm, table_hbm, index_hbm, scale_ref,
    out_hbm,
    region_ref, wqkv_ref, wproj_ref, wfc1_ref, wfc2_ref, gain1_ref, gain2_ref, table_ref, index_ref,
    raw, T, X, A, R, O, GQ, GP, GF, WQ, WP, W1, W2,
    QKV, M, bias, tab, RS, RT, LB, FQ, FK, tmp,
    raw_sem, in_sem, out_sem, z_send, z_recv, g_send, g_recv, d_send, d_recv, h_send, h_recv, r_send, r_recv,
):
    row, col = lax.axis_index("row"), lax.axis_index("col")
    core = row & 1
    at = (row >> 2, col >> 1, (row & 2) + (col & 1))

    def chip(x, y, z, c):
        return {"row": x * 4 + (z & 2) + c, "col": y * 2 + (z & 1)}

    def near(dr, dc):
        return {"row": (row + dr + 16) & 15, "col": (col + dc + 8) & 7}

    def along(axis, step):
        spot = list(at)
        spot[axis] = (spot[axis] + step) & 3
        return chip(*spot, core)

    sibling = chip(*at, 1 - core)
    peers = [along(axis, step) for axis in range(3) for step in (1, 2, 3)] + [sibling]
    peers += [near(-1, 0), near(1, 0), near(0, -1), near(0, 1), near(-1, -1), near(1, 1)]
    barrier = pltpu.get_barrier_semaphore()
    for peer in peers:
        pl.semaphore_signal(barrier, inc=1, device_id=peer, device_id_type=MESH)

    inputs = [
        pltpu.make_async_copy(source, dest, in_sem.at[n])
        for n, (source, dest) in enumerate((
            (wqkv_hbm, wqkv_ref), (wproj_hbm, wproj_ref), (region_hbm, region_ref), (wfc1_hbm, wfc1_ref),
            (wfc2_hbm, wfc2_ref), (table_hbm, table_ref), (index_hbm, index_ref), (gain1_hbm, gain1_ref), (gain2_hbm, gain2_ref),
        ))
    ]
    loads = [pltpu.make_async_copy(tok_hbm.at[i], raw.at[i], raw_sem.at[i]) for i in range(2)]
    for copy in inputs + loads:
        copy.start()
    for copy in inputs:
        copy.wait()

    here = (core, at[0], at[1], at[2])
    for flow in range(3):
        GQ[here + (slice(None), slice(128 * flow, 128 * flow + 128))] = own_block(wqkv_ref, 512 * flow, 128, tmp)
    GP[here] = own_block(wproj_ref, 0, 128, tmp)
    GF[here + (slice(None), slice(0, 512))] = own_block(wfc1_ref, 0, 512, tmp)
    GF[here + (slice(None), slice(512, 1024))] = wfc2_ref[...]
    RS[0] = jnp.zeros((16, 128), jnp.int32)
    RS[0, :, 0:48] = region_ref[...]

    for image in range(2):
        loads[image].wait()
        for half in (image, 1 - image):
            rows = raw[image, 8 * half : 8 * half + 8].astype(F32)
            for group in range(6):
                part = rows[:, 8 * group : 8 * group + 8, :].reshape(64, 512).astype(BF)
                T[image, half, group] = part
                if image == 0 and half == 1 and group > 0:
                    X[0, 0, group - 1] = part
                if image == 1 and half == 0 and group < 5:
                    X[1, 1, group + 1] = part

    pl.semaphore_wait(barrier, len(peers))

    sends = []

    def send(src, dst, s_sem, r_sem, device):
        copy = pltpu.make_async_remote_copy(
            src_ref=src, dst_ref=dst, send_sem=s_sem, recv_sem=r_sem,
            device_id=device, device_id_type=MESH,
        )
        copy.start()
        sends.append(copy)
        return copy

    batches = (GQ, GP, GF)

    def step_z(batch):
        part = batches[batch].at[here]
        return [send(part, part, z_send.at[batch, t - 1], z_recv.at[batch, t - 1], along(2, t)) for t in (1, 3, 2)]

    def slab(batch, flow, step, shift=0):
        spot = list(at[:2])
        axis = ROUTES[flow][step]
        spot[axis] = (spot[axis] + shift) & 3
        if step == 1:
            spot[ROUTES[flow][0]] = slice(None)
        return batches[batch].at[core, spot[0], spot[1], 2 * flow : 2 * flow + 2]

    def step_xy(batch, step, before):
        copies = {}
        if step == 0:
            for copy in before:
                copy.wait_recv()
        for flow in range(2):
            if step == 1:
                for copy in before[flow]:
                    copy.wait_recv()
            part = slab(batch, flow, step)
            copies[flow] = [
                send(part, part, g_send.at[batch, flow, step, t - 1], g_recv.at[batch, flow, step, t - 1],
                     along(ROUTES[flow][step], t))
                for t in (1, 3, 2)
            ]
        return copies

    def across(batch, flow, piece):
        part = slab(batch, flow, 1, piece)
        return send(part, part, d_send.at[batch, flow, piece], d_recv.at[batch, flow, piece], sibling)

    def pass_on(batch, final, orders=(0, 1, 2)):
        crossed = []
        for order in orders:
            for flow in range(2):
                final[flow][order].wait_recv()
                crossed.append(across(batch, flow, (3, 1, 2)[order]))
        return crossed

    qkv = step_z(0)
    halo = [
        send(RS.at[0], RS.at[1], h_send.at[6], h_recv.at[6], near(1, 0)),
        send(RS.at[0], RS.at[2], h_send.at[7], h_recv.at[7], near(1, 1)),
        send(T.at[0, 0, 1:6], X.at[0, 1, 0:5], h_send.at[0], h_recv.at[0], near(-1, 0)),
        send(T.at[0, 0, 0], X.at[0, 1, 5], h_send.at[1], h_recv.at[1], near(-1, -1)),
        send(T.at[0, 1, 0], X.at[0, 0, 5], h_send.at[2], h_recv.at[2], near(0, -1)),
        send(T.at[1, 1, 0:5], X.at[1, 0, 1:6], h_send.at[3], h_recv.at[3], near(1, 0)),
        send(T.at[1, 1, 5], X.at[1, 0, 0], h_send.at[4], h_recv.at[4], near(1, 1)),
        send(T.at[1, 0, 5], X.at[1, 1, 0], h_send.at[5], h_recv.at[5], near(0, 1)),
    ]
    proj = step_z(1)
    fc = step_z(2)

    levels = jnp.round((2048.0 * 16.0 * LOG2E) * jax.nn.sigmoid(table_ref[...])).astype(jnp.int32)
    pairs = levels[0:8] + (levels[8:16] - 32768) * 65536
    for chunk in range(7):
        tab[chunk] = pairs[:, 128 * chunk : 128 * chunk + 128]
    tab[7, :, 0:65] = pairs[:, 896:961]
    lane = iota((8, 128), 1)
    reorder = (lane // 8 % 8) * 16 + (lane // 64) * 8 + lane % 8

    def bias_rows(start, stop):
        def one(n, carry):
            source = (n // 16) * 128 + (n % 8) * 16 + (n // 8 % 2) * 8
            to = pl.ds(pl.multiple_of(n * 8, 8), 8)
            for half in range(2):
                lanes = slice(128 * half, 128 * half + 128)
                index = index_ref[pl.ds(pl.multiple_of(source, 8), 8), lanes]
                index = jnp.take_along_axis(index, reorder, axis=1, mode="promise_in_bounds")
                high, low = index // 128, index % 128
                for head in range(8):
                    found = jnp.zeros((8, 128), jnp.int32)
                    for chunk in range(8):
                        entry = jnp.broadcast_to(tab[chunk, head : head + 1, :], (8, 128))
                        value = jnp.take_along_axis(entry, low, axis=1, mode="promise_in_bounds")
                        found = jnp.where(high == chunk, value, found)
                    bias[head, to, lanes] = (found & 65535).astype(F32) * (1.0 / 2048.0)
                    bias[head + 8, to, lanes] = (found >> 16).astype(F32) * (1.0 / 2048.0) + 16.0
            return carry

        lax.fori_loop(start, stop, one, 0)

    bias_rows(0, 8)
    qkv = step_xy(0, 0, qkv)
    bias_rows(8, 20)
    qkv = step_xy(0, 1, qkv)
    crossed = [across(0, flow, 0) for flow in range(2)]
    proj = step_xy(1, 0, proj)
    bias_rows(20, 32)

    for copy in halo[:2]:
        copy.wait_recv()
    for place in range(3):
        RT[place] = RS[place].astype(F32).T

    o, i = iota((256, 256), 0), iota((256, 256), 1)
    spot = (o // 8 % 4) * 64 + (o // 32 % 2) * 32 + (o // 4 % 2) * 16 + (o // 64) * 4 + o % 4
    permute = jnp.where(spot == i, 1.0, 0.0).astype(BF)
    squares = jnp.where(o // 32 == i // 32, 1.0, 0.0).astype(BF)

    def natural(source, first, lanes, dests, unroll):
        def one(n, carry):
            c, x = n // 4, n % 4
            block = source[c, x, :, :, :, first : first + lanes * len(dests)].reshape(256, lanes * len(dests))
            found = jnp.dot(permute, block, preferred_element_type=F32).astype(BF)
            for k, dest in enumerate(dests):
                for quarter in range(4):
                    for high in range(2):
                        base = 64 * quarter + 32 * high
                        to = pl.multiple_of(x * 128 + high * 64 + c * 32, 32)
                        dest[pl.ds(to, 32), lanes * quarter : lanes * quarter + lanes] = found[
                            base : base + 32, lanes * k : lanes * k + lanes
                        ]
            return carry

        lax.fori_loop(0, 8, one, 0, unroll=unroll)

    crossed += pass_on(0, qkv, (0,))
    fc = step_xy(2, 0, fc)
    crossed += pass_on(0, qkv, (1, 2))
    proj = step_xy(1, 1, proj)
    crossed_proj = [across(1, flow, 0) for flow in range(2)]
    for copy in crossed:
        copy.wait_recv()
    natural(GQ, 0, 128, [WQ.at[flow] for flow in range(3)], True)

    lane512 = iota((1, 512), 1)
    scale = jnp.zeros((1, 512), F32)
    for head in range(16):
        scale = jnp.where(lane512 // 32 == head, scale_ref[head] * LOG2E, scale)

    def project(image, upper):
        x = X[image, upper].reshape(384, 512)
        for kind in range(3):
            value = jnp.dot(x, WQ[kind], preferred_element_type=F32)
            if kind < 2:
                square = (value * value).astype(BF)
                length = jnp.concatenate(
                    [jnp.dot(square[:, 256 * s : 256 * s + 256], squares, preferred_element_type=F32) for s in range(2)], 1)
                unit = lax.rsqrt(jnp.maximum(length, 1.0))
                value = value * (unit * scale if kind == 0 else unit)
            value = value.astype(BF)
            for j in range(3):
                for block in range(4):
                    QKV[3 * image + j, kind, block, 128 * upper : 128 * upper + 128] = value[
                        128 * j : 128 * j + 128, 128 * block : 128 * block + 128
                    ]

    side = {0: halo[4], 1: halo[7]}
    for image in range(2):
        side[image].wait_recv()
        project(image, image)
    fc = step_xy(2, 1, fc)
    crossed = [across(2, flow, 0) for flow in range(2)]
    crossed_proj += pass_on(1, proj)
    for image in range(2):
        for copy in halo[2 + 3 * image : 4 + 3 * image]:
            copy.wait_recv()
        project(image, 1 - image)

    lane128 = iota((1, 128), 1)
    ones = jnp.ones((256, 128), BF)

    def attend(image, j):
        w = 3 * image + j
        place, start = (0, 16 * j) if image == 0 else ((2, 32) if j == 0 else (1, 16 * (j - 1)))
        for n in range(32):
            a, b = (n // 16) * 8 + n % 8, n // 8 % 2
            LB[8 * n : 8 * n + 8] = jnp.broadcast_to(RT[place, start + 8 * b : start + 8 * b + 8, a : a + 1], (8, 128))
        label = LB[...]
        for i in range(4):
            m = lane128 - 32 * ((i + 1) % 4)
            target = jnp.where((m >= 0) & (m < 6), m % 3, -1).astype(F32)
            hi, lo = 144.0, 100.0 * LOG2E - 144.0
            big = jnp.where(m < 3, hi, lo)
            rest = jnp.where(m == 6, -hi, jnp.where(m == 7, -lo, 0.0))
            unit = jnp.where((m == 6) | (m == 7), 1.0, 0.0)
            same = label == target
            FQ[i] = jnp.where(same, big, rest).astype(BF)
            FK[i] = jnp.where(same, 1.0, unit).astype(BF)

        for block in range(4):
            q, k = QKV[w, 0, block], QKV[w, 1, block]
            v = jnp.concatenate([QKV[w, 2, block], ones], 1)
            top = jnp.zeros((256, 128), F32)
            total = jnp.zeros((256, 128), F32)
            for i in range(4):
                here = lane128 // 32 == i
                keep = jnp.where(here, 1.0, 0.0).astype(BF)
                qh = q * keep + FQ[i]
                kh = k * keep + FK[i]
                score = lax.dot_general(qh, kh, (((1,), (1,)), ((), ())), preferred_element_type=F32)
                weight = jnp.exp2(score + bias[4 * block + i]).astype(BF)
                found = jnp.dot(weight, v, preferred_element_type=F32)
                top = jnp.where(here, found[:, :128], top)
                total = jnp.where(here, found[:, 128:], total)
            M[block] = (top / total).astype(BF)
        mixed = jnp.concatenate([M[b] for b in range(4)], 1)
        done = jnp.dot(mixed, WP[...], preferred_element_type=F32).astype(BF).reshape(2, 2, 64, 512)
        for upper in range(2):
            for right in range(2):
                g = 2 * j + right
                if image == 0 and upper == 0 and g < 5:
                    R[0, 1, g + 1] = done[upper, right]
                elif image == 1 and upper == 1 and g > 0:
                    R[1, 0, g - 1] = done[upper, right]
                else:
                    A[image, upper, g] = done[upper, right]
        back = []
        for right in range(2):
            g = 2 * j + right
            s = 6 * image + g
            if image == 0:
                dst, to = (R.at[0, 0, g + 1], near(1, 0)) if g < 5 else (R.at[0, 0, 0], near(1, 1))
                back.append(send(A.at[0, 1, g], dst, r_send.at[s], r_recv.at[s], to))
                if g == 5:
                    side_back.append(send(A.at[0, 0, 5], R.at[0, 1, 0], r_send.at[12], r_recv.at[12], near(0, 1)))
            else:
                dst, to = (R.at[1, 1, g - 1], near(-1, 0)) if g > 0 else (R.at[1, 1, 5], near(-1, -1))
                back.append(send(A.at[1, 0, g], dst, r_send.at[s], r_recv.at[s], to))
                if g == 0:
                    side_back.append(send(A.at[1, 1, 0], R.at[1, 0, 5], r_send.at[13], r_recv.at[13], near(0, -1)))
        return back

    def second_rows(n, carry):
        c, x = n // 4, n % 4
        for high in range(2):
            for y in range(4):
                to = pl.multiple_of((x * 32 + high * 16 + c * 8 + y * 2) * 16, 32)
                W2[pl.ds(to, 32)] = GF[c, x, y, 2 * high : 2 * high + 2, :, 512:1024].reshape(32, 512)
        return carry

    back = {0: [], 1: []}
    side_back = []
    for copy in crossed_proj:
        copy.wait_recv()
    natural(GP, 0, 128, [WP], True)
    for n, (image, j) in enumerate(((0, 2), (0, 0), (0, 1), (1, 0), (1, 1), (1, 2))):
        back[image] += attend(image, j)
        if n >= 3:
            crossed += pass_on(2, fc, (n - 3,))
    for copy in crossed:
        copy.wait_recv()
    natural(GF, 0, 512, [W1], 4)
    lax.fori_loop(0, 8, second_rows, 0)

    def mlp(image, half):
        after = T[image, half].reshape(384, 512).astype(F32)
        after = after + layer_norm(R[image, half].reshape(384, 512).astype(F32), gain1_ref[...])
        after = after.astype(BF)
        units = []
        for part in range(4):
            hidden = jnp.dot(after, W1[:, 512 * part : 512 * part + 512], preferred_element_type=F32)
            units.append((0.5 * hidden * (1.0 + lax.erf(hidden * math.sqrt(0.5)))).astype(BF))
        total = jnp.dot(jnp.concatenate(units, 1), W2[...], preferred_element_type=F32)
        result = after.astype(F32) + layer_norm(total, gain2_ref[...])
        result = result.reshape(6, 8, 8, 512)
        O[image, half] = jnp.concatenate([result[g] for g in range(6)], 1).astype(BF)
        copy = pltpu.make_async_copy(O.at[image, half], out_hbm.at[image, 8 * half : 8 * half + 8], out_sem.at[image, half])
        copy.start()
        return copy

    outs = []
    for image in range(2):
        side_back[image].wait_recv()
        outs.append(mlp(image, 1 - image))
        for copy in back[image]:
            copy.wait_recv()
        outs.append(mlp(image, image))
    for copy in sends:
        copy.wait_send()
    for copy in outs:
        copy.wait()


def body(
    tokens, region, w_qkv, w_proj, w_fc1, w_fc2, gain_attn, gain_mlp, table, index, logit_scale
):
    DMA = pltpu.SemaphoreType.DMA
    V = pltpu.VMEM
    tiles = (2, 2, 6, 64, 512)
    return pl.pallas_call(
        kernel,
        out_shape=jax.ShapeDtypeStruct((2, 16, 48, 512), BF),
        in_specs=[pl.BlockSpec(memory_space=pl.ANY)] * 10 + [pl.BlockSpec(memory_space=pltpu.SMEM)],
        out_specs=pl.BlockSpec(memory_space=pl.ANY),
        scratch_shapes=[
            V((16, 48), jnp.int32), V((4, 1536), BF), V((4, 512), BF), V((4, 2048), BF), V((16, 512), BF),
            V((1, 512), F32), V((1, 512), F32), V((16, 961), F32), V((256, 256), jnp.int32),
            V((2, 16, 48, 512), BF), V(tiles, BF), V(tiles, BF), V(tiles, BF), V(tiles, BF), V((2, 2, 8, 48, 512), BF),
            V((2, 4, 4, 4, 16, 384), BF), V((2, 4, 4, 4, 16, 128), BF), V((2, 4, 4, 4, 16, 1024), BF),
            V((3, 512, 512), BF), V((512, 512), BF), V((512, 2048), BF), V((2048, 512), BF),
            V((6, 3, 4, 256, 128), BF), V((4, 256, 128), BF), V((16, 256, 256), F32), V((8, 8, 128), jnp.int32),
            V((3, 16, 128), jnp.int32), V((3, 128, 16), F32), V((256, 128), F32),
            V((4, 256, 128), BF), V((4, 256, 128), BF), V((16, 512), F32),
            DMA((2,)), DMA((9,)), DMA((2, 2)), DMA((3, 3)), DMA((3, 3)), DMA((3, 2, 2, 3)), DMA((3, 2, 2, 3)), DMA((3, 2, 4)), DMA((3, 2, 4)),
            DMA((8,)), DMA((8,)), DMA((14,)), DMA((14,)),
        ],
        compiler_params=pltpu.CompilerParams(
            collective_id=0, has_side_effects=True, vmem_limit_bytes=60 * 1024 * 1024
        ),
    )(
        tokens, region, w_qkv, w_proj, w_fc1, w_fc2,
        gain_attn.reshape(1, 512), gain_mlp.reshape(1, 512), table.T, index, logit_scale,
    )


def solution(mesh):
    split = P(("row", "col"), None)
    return jax.shard_map(
        body,
        mesh=mesh,
        in_specs=(P(None, "row", "col", None), P("row", "col"), split, split, split, split, P(), P(), P(), P(), P()),
        out_specs=P(None, "row", "col", None),
        check_vma=False,
    )
```

```python
import math

import jax
import jax.numpy as jnp
from jax import lax
from jax.experimental import pallas as pl
from jax.experimental.pallas import tpu as pltpu
from jax.sharding import PartitionSpec as P

MESH = pl.DeviceIdType.MESH
BF = jnp.bfloat16
F32 = jnp.float32
LOG2E = math.log2(math.e)
ROUTES = ((1, 0), (0, 1))


def iota(shape, dim):
    return lax.broadcasted_iota(jnp.int32, shape, dim)


def layer_norm(value, gain):
    mean = jnp.mean(value, -1, keepdims=True)
    centered = value - mean
    variance = jnp.mean(centered * centered, -1, keepdims=True)
    return centered * lax.rsqrt(variance + 1e-05) * gain


def own_block(w_ref, lo, lanes, tmp):
    for quarter in range(4):
        at = lo + quarter * lanes
        tmp[4 * quarter : 4 * quarter + 4, :lanes] = w_ref[:, at : at + lanes].astype(F32)
    return tmp[:, :lanes].astype(BF)


def kernel(
    tok_hbm, region_hbm, wqkv_hbm, wproj_hbm, wfc1_hbm, wfc2_hbm,
    gain1_hbm, gain2_hbm, table_hbm, index_hbm, scale_ref,
    out_hbm,
    region_ref, wqkv_ref, wproj_ref, wfc1_ref, wfc2_ref, gain1_ref, gain2_ref, table_ref, index_ref,
    raw, T, X, A, R, O, GQ, GP, GF, WQ, WP, W1, W2,
    QKV, M, bias, tab, RS, RT, LB, FQ, FK, tmp,
    raw_sem, in_sem, out_sem, z_send, z_recv, g_send, g_recv, d_send, d_recv, h_send, h_recv, r_send, r_recv,
):
    row, col = lax.axis_index("row"), lax.axis_index("col")
    core = row & 1
    at = (row >> 2, col >> 1, (row & 2) + (col & 1))

    def chip(x, y, z, c):
        return {"row": x * 4 + (z & 2) + c, "col": y * 2 + (z & 1)}

    def near(dr, dc):
        return {"row": (row + dr + 16) & 15, "col": (col + dc + 8) & 7}

    def along(axis, step):
        spot = list(at)
        spot[axis] = (spot[axis] + step) & 3
        return chip(*spot, core)

    sibling = chip(*at, 1 - core)
    peers = [along(axis, step) for axis in range(3) for step in (1, 2, 3)] + [sibling]
    peers += [near(-1, 0), near(1, 0), near(0, -1), near(0, 1), near(-1, -1), near(1, 1)]
    barrier = pltpu.get_barrier_semaphore()
    for peer in peers:
        pl.semaphore_signal(barrier, inc=1, device_id=peer, device_id_type=MESH)

    inputs = [
        pltpu.make_async_copy(source, dest, in_sem.at[n])
        for n, (source, dest) in enumerate((
            (wqkv_hbm, wqkv_ref), (wproj_hbm, wproj_ref), (region_hbm, region_ref), (wfc1_hbm, wfc1_ref),
            (wfc2_hbm, wfc2_ref), (table_hbm, table_ref), (index_hbm, index_ref), (gain1_hbm, gain1_ref), (gain2_hbm, gain2_ref),
        ))
    ]
    loads = [pltpu.make_async_copy(tok_hbm.at[i], raw.at[i], raw_sem.at[i]) for i in range(2)]
    for copy in inputs + loads:
        copy.start()
    for copy in inputs:
        copy.wait()

    here = (core, at[0], at[1], at[2])
    for flow in range(3):
        GQ[here + (slice(None), slice(128 * flow, 128 * flow + 128))] = own_block(wqkv_ref, 512 * flow, 128, tmp)
    GP[here] = own_block(wproj_ref, 0, 128, tmp)
    GF[here + (slice(None), slice(0, 512))] = own_block(wfc1_ref, 0, 512, tmp)
    GF[here + (slice(None), slice(512, 1024))] = wfc2_ref[...]
    RS[0] = jnp.zeros((16, 128), jnp.int32)
    RS[0, :, 0:48] = region_ref[...]

    for image in range(2):
        loads[image].wait()
        for half in (image, 1 - image):
            rows = raw[image, 8 * half : 8 * half + 8].astype(F32)
            for group in range(6):
                part = rows[:, 8 * group : 8 * group + 8, :].reshape(64, 512).astype(BF)
                T[image, half, group] = part
                if image == 0 and half == 1 and group > 0:
                    X[0, 0, group - 1] = part
                if image == 1 and half == 0 and group < 5:
                    X[1, 1, group + 1] = part

    pl.semaphore_wait(barrier, len(peers))

    sends = []

    def send(src, dst, s_sem, r_sem, device):
        copy = pltpu.make_async_remote_copy(
            src_ref=src, dst_ref=dst, send_sem=s_sem, recv_sem=r_sem,
            device_id=device, device_id_type=MESH,
        )
        copy.start()
        sends.append(copy)
        return copy

    batches = (GQ, GP, GF)

    def step_z(batch):
        part = batches[batch].at[here]
        return [send(part, part, z_send.at[batch, t - 1], z_recv.at[batch, t - 1], along(2, t)) for t in (1, 3, 2)]

    def slab(batch, flow, step, shift=0):
        spot = list(at[:2])
        axis = ROUTES[flow][step]
        spot[axis] = (spot[axis] + shift) & 3
        if step == 1:
            spot[ROUTES[flow][0]] = slice(None)
        return batches[batch].at[core, spot[0], spot[1], 2 * flow : 2 * flow + 2]

    def step_xy(batch, step, before):
        copies = {}
        if step == 0:
            for copy in before:
                copy.wait_recv()
        for flow in range(2):
            if step == 1:
                for copy in before[flow]:
                    copy.wait_recv()
            part = slab(batch, flow, step)
            copies[flow] = [
                send(part, part, g_send.at[batch, flow, step, t - 1], g_recv.at[batch, flow, step, t - 1],
                     along(ROUTES[flow][step], t))
                for t in (1, 3, 2)
            ]
        return copies

    def across(batch, flow, piece):
        part = slab(batch, flow, 1, piece)
        return send(part, part, d_send.at[batch, flow, piece], d_recv.at[batch, flow, piece], sibling)

    def pass_on(batch, final, orders=(0, 1, 2)):
        crossed = []
        for order in orders:
            for flow in range(2):
                final[flow][order].wait_recv()
                crossed.append(across(batch, flow, (3, 1, 2)[order]))
        return crossed

    qkv, proj, fc = step_z(0), step_z(1), step_z(2)
    halo = [
        send(RS.at[0], RS.at[1], h_send.at[6], h_recv.at[6], near(1, 0)),
        send(RS.at[0], RS.at[2], h_send.at[7], h_recv.at[7], near(1, 1)),
        send(T.at[0, 0, 1:6], X.at[0, 1, 0:5], h_send.at[0], h_recv.at[0], near(-1, 0)),
        send(T.at[0, 0, 0], X.at[0, 1, 5], h_send.at[1], h_recv.at[1], near(-1, -1)),
        send(T.at[0, 1, 0], X.at[0, 0, 5], h_send.at[2], h_recv.at[2], near(0, -1)),
        send(T.at[1, 1, 0:5], X.at[1, 0, 1:6], h_send.at[3], h_recv.at[3], near(1, 0)),
        send(T.at[1, 1, 5], X.at[1, 0, 0], h_send.at[4], h_recv.at[4], near(1, 1)),
        send(T.at[1, 0, 5], X.at[1, 1, 0], h_send.at[5], h_recv.at[5], near(0, 1)),
    ]

    levels = jnp.round((2048.0 * 16.0 * LOG2E) * jax.nn.sigmoid(table_ref[...])).astype(jnp.int32)
    pairs = levels[0:8] + (levels[8:16] - 32768) * 65536
    for chunk in range(7):
        tab[chunk] = pairs[:, 128 * chunk : 128 * chunk + 128]
    tab[7, :, 0:65] = pairs[:, 896:961]
    lane = iota((8, 128), 1)
    reorder = (lane // 8 % 8) * 16 + (lane // 64) * 8 + lane % 8

    def bias_rows(start, stop):
        def one(n, carry):
            source = (n // 16) * 128 + (n % 8) * 16 + (n // 8 % 2) * 8
            to = pl.ds(pl.multiple_of(n * 8, 8), 8)
            for half in range(2):
                lanes = slice(128 * half, 128 * half + 128)
                index = index_ref[pl.ds(pl.multiple_of(source, 8), 8), lanes]
                index = jnp.take_along_axis(index, reorder, axis=1, mode="promise_in_bounds")
                high, low = index // 128, index % 128
                for head in range(8):
                    found = jnp.zeros((8, 128), jnp.int32)
                    for chunk in range(8):
                        entry = jnp.broadcast_to(tab[chunk, head : head + 1, :], (8, 128))
                        value = jnp.take_along_axis(entry, low, axis=1, mode="promise_in_bounds")
                        found = jnp.where(high == chunk, value, found)
                    bias[head, to, lanes] = (found & 65535).astype(F32) * (1.0 / 2048.0)
                    bias[head + 8, to, lanes] = (found >> 16).astype(F32) * (1.0 / 2048.0) + 16.0
            return carry

        lax.fori_loop(start, stop, one, 0)

    bias_rows(0, 8)
    qkv = step_xy(0, 0, qkv)
    proj = step_xy(1, 0, proj)
    bias_rows(8, 14)
    fc = step_xy(2, 0, fc)
    bias_rows(14, 20)
    qkv = step_xy(0, 1, qkv)
    crossed = [across(0, flow, 0) for flow in range(2)]
    bias_rows(20, 32)

    for copy in halo[:2]:
        copy.wait_recv()
    for place in range(3):
        RT[place] = RS[place].astype(F32).T

    o, i = iota((256, 256), 0), iota((256, 256), 1)
    spot = (o // 8 % 4) * 64 + (o // 32 % 2) * 32 + (o // 4 % 2) * 16 + (o // 64) * 4 + o % 4
    permute = jnp.where(spot == i, 1.0, 0.0).astype(BF)
    squares = jnp.where(o // 32 == i // 32, 1.0, 0.0).astype(BF)

    def natural(source, first, lanes, dests, unroll):
        def one(n, carry):
            c, x = n // 4, n % 4
            block = source[c, x, :, :, :, first : first + lanes * len(dests)].reshape(256, lanes * len(dests))
            found = jnp.dot(permute, block, preferred_element_type=F32).astype(BF)
            for k, dest in enumerate(dests):
                for quarter in range(4):
                    for high in range(2):
                        base = 64 * quarter + 32 * high
                        to = pl.multiple_of(x * 128 + high * 64 + c * 32, 32)
                        dest[pl.ds(to, 32), lanes * quarter : lanes * quarter + lanes] = found[
                            base : base + 32, lanes * k : lanes * k + lanes
                        ]
            return carry

        lax.fori_loop(0, 8, one, 0, unroll=unroll)

    crossed += pass_on(0, qkv, (0,))
    proj = step_xy(1, 1, proj)
    fc = step_xy(2, 1, fc)
    crossed += pass_on(0, qkv, (1, 2))
    crossed_proj = [across(1, flow, 0) for flow in range(2)]
    for copy in crossed:
        copy.wait_recv()
    natural(GQ, 0, 128, [WQ.at[flow] for flow in range(3)], True)

    lane512 = iota((1, 512), 1)
    scale = jnp.zeros((1, 512), F32)
    for head in range(16):
        scale = jnp.where(lane512 // 32 == head, scale_ref[head] * LOG2E, scale)

    def project(image, upper):
        x = X[image, upper].reshape(384, 512)
        for kind in range(3):
            value = jnp.dot(x, WQ[kind], preferred_element_type=F32)
            if kind < 2:
                square = (value * value).astype(BF)
                length = jnp.concatenate(
                    [jnp.dot(square[:, 256 * s : 256 * s + 256], squares, preferred_element_type=F32) for s in range(2)], 1)
                unit = lax.rsqrt(jnp.maximum(length, 1.0))
                value = value * (unit * scale if kind == 0 else unit)
            value = value.astype(BF)
            for j in range(3):
                for block in range(4):
                    QKV[3 * image + j, kind, block, 128 * upper : 128 * upper + 128] = value[
                        128 * j : 128 * j + 128, 128 * block : 128 * block + 128
                    ]

    side = {0: halo[4], 1: halo[7]}
    for image in range(2):
        side[image].wait_recv()
        project(image, image)
    crossed = [across(2, flow, 0) for flow in range(2)]
    crossed_proj += pass_on(1, proj)
    for image in range(2):
        for copy in halo[2 + 3 * image : 4 + 3 * image]:
            copy.wait_recv()
        project(image, 1 - image)

    lane128 = iota((1, 128), 1)
    ones = jnp.ones((256, 128), BF)

    def attend(image, j):
        w = 3 * image + j
        place, start = (0, 16 * j) if image == 0 else ((2, 32) if j == 0 else (1, 16 * (j - 1)))
        for n in range(32):
            a, b = (n // 16) * 8 + n % 8, n // 8 % 2
            LB[8 * n : 8 * n + 8] = jnp.broadcast_to(RT[place, start + 8 * b : start + 8 * b + 8, a : a + 1], (8, 128))
        label = LB[...]
        for i in range(4):
            m = lane128 - 32 * ((i + 1) % 4)
            target = jnp.where((m >= 0) & (m < 6), m % 3, -1).astype(F32)
            hi, lo = 144.0, 100.0 * LOG2E - 144.0
            big = jnp.where(m < 3, hi, lo)
            rest = jnp.where(m == 6, -hi, jnp.where(m == 7, -lo, 0.0))
            unit = jnp.where((m == 6) | (m == 7), 1.0, 0.0)
            same = label == target
            FQ[i] = jnp.where(same, big, rest).astype(BF)
            FK[i] = jnp.where(same, 1.0, unit).astype(BF)

        for block in range(4):
            q, k = QKV[w, 0, block], QKV[w, 1, block]
            v = jnp.concatenate([QKV[w, 2, block], ones], 1)
            top = jnp.zeros((256, 128), F32)
            total = jnp.zeros((256, 128), F32)
            for i in range(4):
                here = lane128 // 32 == i
                keep = jnp.where(here, 1.0, 0.0).astype(BF)
                qh = q * keep + FQ[i]
                kh = k * keep + FK[i]
                score = lax.dot_general(qh, kh, (((1,), (1,)), ((), ())), preferred_element_type=F32)
                weight = jnp.exp2(score + bias[4 * block + i]).astype(BF)
                found = jnp.dot(weight, v, preferred_element_type=F32)
                top = jnp.where(here, found[:, :128], top)
                total = jnp.where(here, found[:, 128:], total)
            M[block] = (top / total).astype(BF)
        mixed = jnp.concatenate([M[b] for b in range(4)], 1)
        done = jnp.dot(mixed, WP[...], preferred_element_type=F32).astype(BF).reshape(2, 2, 64, 512)
        for upper in range(2):
            for right in range(2):
                g = 2 * j + right
                if image == 0 and upper == 0 and g < 5:
                    R[0, 1, g + 1] = done[upper, right]
                elif image == 1 and upper == 1 and g > 0:
                    R[1, 0, g - 1] = done[upper, right]
                else:
                    A[image, upper, g] = done[upper, right]
        back = []
        for right in range(2):
            g = 2 * j + right
            s = 6 * image + g
            if image == 0:
                dst, to = (R.at[0, 0, g + 1], near(1, 0)) if g < 5 else (R.at[0, 0, 0], near(1, 1))
                back.append(send(A.at[0, 1, g], dst, r_send.at[s], r_recv.at[s], to))
                if g == 5:
                    side_back.append(send(A.at[0, 0, 5], R.at[0, 1, 0], r_send.at[12], r_recv.at[12], near(0, 1)))
            else:
                dst, to = (R.at[1, 1, g - 1], near(-1, 0)) if g > 0 else (R.at[1, 1, 5], near(-1, -1))
                back.append(send(A.at[1, 0, g], dst, r_send.at[s], r_recv.at[s], to))
                if g == 0:
                    side_back.append(send(A.at[1, 1, 0], R.at[1, 0, 5], r_send.at[13], r_recv.at[13], near(0, -1)))
        return back

    def second_rows(n, carry):
        c, x = n // 4, n % 4
        for high in range(2):
            for y in range(4):
                to = pl.multiple_of((x * 32 + high * 16 + c * 8 + y * 2) * 16, 32)
                W2[pl.ds(to, 32)] = GF[c, x, y, 2 * high : 2 * high + 2, :, 512:1024].reshape(32, 512)
        return carry

    back = {0: [], 1: []}
    side_back = []
    for copy in crossed_proj:
        copy.wait_recv()
    natural(GP, 0, 128, [WP], True)
    for n, (image, j) in enumerate(((0, 2), (0, 0), (0, 1), (1, 0), (1, 1), (1, 2))):
        back[image] += attend(image, j)
        if n in (2, 3, 4):
            crossed += pass_on(2, fc, (n - 2,))
    for copy in crossed:
        copy.wait_recv()
    natural(GF, 0, 512, [W1], 4)
    lax.fori_loop(0, 8, second_rows, 0)

    def mlp(image, half):
        after = T[image, half].reshape(384, 512).astype(F32)
        after = after + layer_norm(R[image, half].reshape(384, 512).astype(F32), gain1_ref[...])
        after = after.astype(BF)
        units = []
        for part in range(4):
            hidden = jnp.dot(after, W1[:, 512 * part : 512 * part + 512], preferred_element_type=F32)
            units.append((0.5 * hidden * (1.0 + lax.erf(hidden * math.sqrt(0.5)))).astype(BF))
        total = jnp.dot(jnp.concatenate(units, 1), W2[...], preferred_element_type=F32)
        result = after.astype(F32) + layer_norm(total, gain2_ref[...])
        result = result.reshape(6, 8, 8, 512)
        O[image, half] = jnp.concatenate([result[g] for g in range(6)], 1).astype(BF)
        copy = pltpu.make_async_copy(O.at[image, half], out_hbm.at[image, 8 * half : 8 * half + 8], out_sem.at[image, half])
        copy.start()
        return copy

    outs = []
    for image in range(2):
        side_back[image].wait_recv()
        outs.append(mlp(image, 1 - image))
        for copy in back[image]:
            copy.wait_recv()
        outs.append(mlp(image, image))
    for copy in sends:
        copy.wait_send()
    for copy in outs:
        copy.wait()


def body(
    tokens, region, w_qkv, w_proj, w_fc1, w_fc2, gain_attn, gain_mlp, table, index, logit_scale
):
    DMA = pltpu.SemaphoreType.DMA
    V = pltpu.VMEM
    tiles = (2, 2, 6, 64, 512)
    return pl.pallas_call(
        kernel,
        out_shape=jax.ShapeDtypeStruct((2, 16, 48, 512), BF),
        in_specs=[pl.BlockSpec(memory_space=pl.ANY)] * 10 + [pl.BlockSpec(memory_space=pltpu.SMEM)],
        out_specs=pl.BlockSpec(memory_space=pl.ANY),
        scratch_shapes=[
            V((16, 48), jnp.int32), V((4, 1536), BF), V((4, 512), BF), V((4, 2048), BF), V((16, 512), BF),
            V((1, 512), F32), V((1, 512), F32), V((16, 961), F32), V((256, 256), jnp.int32),
            V((2, 16, 48, 512), BF), V(tiles, BF), V(tiles, BF), V(tiles, BF), V(tiles, BF), V((2, 2, 8, 48, 512), BF),
            V((2, 4, 4, 4, 16, 384), BF), V((2, 4, 4, 4, 16, 128), BF), V((2, 4, 4, 4, 16, 1024), BF),
            V((3, 512, 512), BF), V((512, 512), BF), V((512, 2048), BF), V((2048, 512), BF),
            V((6, 3, 4, 256, 128), BF), V((4, 256, 128), BF), V((16, 256, 256), F32), V((8, 8, 128), jnp.int32),
            V((3, 16, 128), jnp.int32), V((3, 128, 16), F32), V((256, 128), F32),
            V((4, 256, 128), BF), V((4, 256, 128), BF), V((16, 512), F32),
            DMA((2,)), DMA((9,)), DMA((2, 2)), DMA((3, 3)), DMA((3, 3)), DMA((3, 2, 2, 3)), DMA((3, 2, 2, 3)), DMA((3, 2, 4)), DMA((3, 2, 4)),
            DMA((8,)), DMA((8,)), DMA((14,)), DMA((14,)),
        ],
        compiler_params=pltpu.CompilerParams(
            collective_id=0, has_side_effects=True, vmem_limit_bytes=60 * 1024 * 1024
        ),
    )(
        tokens, region, w_qkv, w_proj, w_fc1, w_fc2,
        gain_attn.reshape(1, 512), gain_mlp.reshape(1, 512), table.T, index, logit_scale,
    )


def solution(mesh):
    split = P(("row", "col"), None)
    return jax.shard_map(
        body,
        mesh=mesh,
        in_specs=(P(None, "row", "col", None), P("row", "col"), split, split, split, split, P(), P(), P(), P(), P()),
        out_specs=P(None, "row", "col", None),
        check_vma=False,
    )
```

```python
import math

import jax
import jax.numpy as jnp
from jax import lax
from jax.experimental import pallas as pl
from jax.experimental.pallas import tpu as pltpu
from jax.sharding import PartitionSpec as P

MESH = pl.DeviceIdType.MESH
BF = jnp.bfloat16
F32 = jnp.float32
LOG2E = math.log2(math.e)
ROUTES = ((1, 0), (0, 1))


def iota(shape, dim):
    return lax.broadcasted_iota(jnp.int32, shape, dim)


def layer_norm(value, gain):
    mean = jnp.mean(value, -1, keepdims=True)
    centered = value - mean
    variance = jnp.mean(centered * centered, -1, keepdims=True)
    return centered * lax.rsqrt(variance + 1e-05) * gain


def own_block(w_ref, lo, lanes, tmp):
    for quarter in range(4):
        at = lo + quarter * lanes
        tmp[4 * quarter : 4 * quarter + 4, :lanes] = w_ref[:, at : at + lanes].astype(F32)
    return tmp[:, :lanes].astype(BF)


def kernel(
    tok_hbm, region_hbm, wqkv_hbm, wproj_hbm, wfc1_hbm, wfc2_hbm,
    gain1_hbm, gain2_hbm, table_hbm, index_hbm, scale_ref,
    out_hbm,
    region_ref, wqkv_ref, wproj_ref, wfc1_ref, wfc2_ref, gain1_ref, gain2_ref, table_ref, index_ref,
    raw, T, X, A, R, O, GQ, GP, GF, WQ, WP, W1, W2,
    QKV, M, bias, tab, RS, RT, LB, FQ, FK, tmp,
    raw_sem, in_sem, out_sem, z_send, z_recv, g_send, g_recv, d_send, d_recv, h_send, h_recv, r_send, r_recv,
):
    row, col = lax.axis_index("row"), lax.axis_index("col")
    core = row & 1
    at = (row >> 2, col >> 1, (row & 2) + (col & 1))

    def chip(x, y, z, c):
        return {"row": x * 4 + (z & 2) + c, "col": y * 2 + (z & 1)}

    def near(dr, dc):
        return {"row": (row + dr + 16) & 15, "col": (col + dc + 8) & 7}

    def along(axis, step):
        spot = list(at)
        spot[axis] = (spot[axis] + step) & 3
        return chip(*spot, core)

    sibling = chip(*at, 1 - core)
    peers = [along(axis, step) for axis in range(3) for step in (1, 2, 3)] + [sibling]
    peers += [near(-1, 0), near(1, 0), near(0, -1), near(0, 1), near(-1, -1), near(1, 1)]
    barrier = pltpu.get_barrier_semaphore()
    for peer in peers:
        pl.semaphore_signal(barrier, inc=1, device_id=peer, device_id_type=MESH)

    inputs = [
        pltpu.make_async_copy(source, dest, in_sem.at[n])
        for n, (source, dest) in enumerate((
            (wqkv_hbm, wqkv_ref), (wproj_hbm, wproj_ref), (region_hbm, region_ref), (wfc1_hbm, wfc1_ref),
            (wfc2_hbm, wfc2_ref), (table_hbm, table_ref), (index_hbm, index_ref), (gain1_hbm, gain1_ref), (gain2_hbm, gain2_ref),
        ))
    ]
    loads = [pltpu.make_async_copy(tok_hbm.at[i], raw.at[i], raw_sem.at[i]) for i in range(2)]
    for copy in inputs + loads:
        copy.start()
    for copy in inputs:
        copy.wait()

    here = (core, at[0], at[1], at[2])
    for flow in range(3):
        GQ[here + (slice(None), slice(128 * flow, 128 * flow + 128))] = own_block(wqkv_ref, 512 * flow, 128, tmp)
    GP[here] = own_block(wproj_ref, 0, 128, tmp)
    GF[here + (slice(None), slice(0, 512))] = own_block(wfc1_ref, 0, 512, tmp)
    GF[here + (slice(None), slice(512, 1024))] = wfc2_ref[...]
    RS[0] = jnp.zeros((16, 128), jnp.int32)
    RS[0, :, 0:48] = region_ref[...]

    for image in range(2):
        loads[image].wait()
        for half in (image, 1 - image):
            rows = raw[image, 8 * half : 8 * half + 8].astype(F32)
            for group in range(6):
                part = rows[:, 8 * group : 8 * group + 8, :].reshape(64, 512).astype(BF)
                T[image, half, group] = part
                if image == 0 and half == 1 and group > 0:
                    X[0, 0, group - 1] = part
                if image == 1 and half == 0 and group < 5:
                    X[1, 1, group + 1] = part

    pl.semaphore_wait(barrier, len(peers))

    sends = []

    def send(src, dst, s_sem, r_sem, device):
        copy = pltpu.make_async_remote_copy(
            src_ref=src, dst_ref=dst, send_sem=s_sem, recv_sem=r_sem,
            device_id=device, device_id_type=MESH,
        )
        copy.start()
        sends.append(copy)
        return copy

    batches = (GQ, GP, GF)

    def step_z(batch):
        part = batches[batch].at[here]
        return [send(part, part, z_send.at[batch, t - 1], z_recv.at[batch, t - 1], along(2, t)) for t in (1, 3, 2)]

    def slab(batch, flow, step, shift=0):
        spot = list(at[:2])
        axis = ROUTES[flow][step]
        spot[axis] = (spot[axis] + shift) & 3
        if step == 1:
            spot[ROUTES[flow][0]] = slice(None)
        return batches[batch].at[core, spot[0], spot[1], 2 * flow : 2 * flow + 2]

    def step_xy(batch, step, before):
        copies = {}
        if step == 0:
            for copy in before:
                copy.wait_recv()
        for flow in range(2):
            if step == 1:
                for copy in before[flow]:
                    copy.wait_recv()
            part = slab(batch, flow, step)
            copies[flow] = [
                send(part, part, g_send.at[batch, flow, step, t - 1], g_recv.at[batch, flow, step, t - 1],
                     along(ROUTES[flow][step], t))
                for t in (1, 3, 2)
            ]
        return copies

    def across(batch, flow, piece):
        part = slab(batch, flow, 1, piece)
        return send(part, part, d_send.at[batch, flow, piece], d_recv.at[batch, flow, piece], sibling)

    def pass_on(batch, final, orders=(0, 1, 2)):
        crossed = []
        for order in orders:
            for flow in range(2):
                final[flow][order].wait_recv()
                crossed.append(across(batch, flow, (3, 1, 2)[order]))
        return crossed

    qkv, proj, fc = step_z(0), step_z(1), step_z(2)
    halo = [
        send(RS.at[0], RS.at[1], h_send.at[6], h_recv.at[6], near(1, 0)),
        send(RS.at[0], RS.at[2], h_send.at[7], h_recv.at[7], near(1, 1)),
        send(T.at[0, 0, 1:6], X.at[0, 1, 0:5], h_send.at[0], h_recv.at[0], near(-1, 0)),
        send(T.at[0, 0, 0], X.at[0, 1, 5], h_send.at[1], h_recv.at[1], near(-1, -1)),
        send(T.at[0, 1, 0], X.at[0, 0, 5], h_send.at[2], h_recv.at[2], near(0, -1)),
        send(T.at[1, 1, 0:5], X.at[1, 0, 1:6], h_send.at[3], h_recv.at[3], near(1, 0)),
        send(T.at[1, 1, 5], X.at[1, 0, 0], h_send.at[4], h_recv.at[4], near(1, 1)),
        send(T.at[1, 0, 5], X.at[1, 1, 0], h_send.at[5], h_recv.at[5], near(0, 1)),
    ]

    levels = jnp.round((2048.0 * 16.0 * LOG2E) * jax.nn.sigmoid(table_ref[...])).astype(jnp.int32)
    pairs = levels[0:8] + (levels[8:16] - 32768) * 65536
    for chunk in range(7):
        tab[chunk] = pairs[:, 128 * chunk : 128 * chunk + 128]
    tab[7, :, 0:65] = pairs[:, 896:961]
    lane = iota((8, 128), 1)
    reorder = (lane // 8 % 8) * 16 + (lane // 64) * 8 + lane % 8

    def bias_rows(start, stop):
        def one(n, carry):
            source = (n // 16) * 128 + (n % 8) * 16 + (n // 8 % 2) * 8
            to = pl.ds(pl.multiple_of(n * 8, 8), 8)
            for half in range(2):
                lanes = slice(128 * half, 128 * half + 128)
                index = index_ref[pl.ds(pl.multiple_of(source, 8), 8), lanes]
                index = jnp.take_along_axis(index, reorder, axis=1, mode="promise_in_bounds")
                high, low = index // 128, index % 128
                for head in range(8):
                    found = jnp.zeros((8, 128), jnp.int32)
                    for chunk in range(8):
                        entry = jnp.broadcast_to(tab[chunk, head : head + 1, :], (8, 128))
                        value = jnp.take_along_axis(entry, low, axis=1, mode="promise_in_bounds")
                        found = jnp.where(high == chunk, value, found)
                    bias[head, to, lanes] = (found & 65535).astype(F32) * (1.0 / 2048.0)
                    bias[head + 8, to, lanes] = (found >> 16).astype(F32) * (1.0 / 2048.0) + 16.0
            return carry

        lax.fori_loop(start, stop, one, 0)

    bias_rows(0, 8)
    qkv = step_xy(0, 0, qkv)
    proj = step_xy(1, 0, proj)
    bias_rows(8, 14)
    fc = step_xy(2, 0, fc)
    bias_rows(14, 20)
    qkv = step_xy(0, 1, qkv)
    crossed = [across(0, flow, 0) for flow in range(2)]
    bias_rows(20, 32)

    for copy in halo[:2]:
        copy.wait_recv()
    for place in range(3):
        RT[place] = RS[place].astype(F32).T

    lane128 = iota((1, 128), 1)

    def mask_lanes(image, j):
        w = 3 * image + j
        place, start = (0, 16 * j) if image == 0 else ((2, 32) if j == 0 else (1, 16 * (j - 1)))
        for n in range(32):
            a, b = (n // 16) * 8 + n % 8, n // 8 % 2
            LB[8 * n : 8 * n + 8] = jnp.broadcast_to(RT[place, start + 8 * b : start + 8 * b + 8, a : a + 1], (8, 128))
        label = LB[...]
        for i in range(4):
            m = lane128 - 32 * ((i + 1) % 4)
            target = jnp.where((m >= 0) & (m < 6), m % 3, -1).astype(F32)
            hi, lo = 144.0, 100.0 * LOG2E - 144.0
            big = jnp.where(m < 3, hi, lo)
            rest = jnp.where(m == 6, -hi, jnp.where(m == 7, -lo, 0.0))
            unit = jnp.where((m == 6) | (m == 7), 1.0, 0.0)
            same = label == target
            FQ[w, i] = jnp.where(same, big, rest).astype(BF)
            FK[w, i] = jnp.where(same, 1.0, unit).astype(BF)

    for w in range(6):
        mask_lanes(w // 3, w % 3)

    o, i = iota((256, 256), 0), iota((256, 256), 1)
    spot = (o // 8 % 4) * 64 + (o // 32 % 2) * 32 + (o // 4 % 2) * 16 + (o // 64) * 4 + o % 4
    permute = jnp.where(spot == i, 1.0, 0.0).astype(BF)
    squares = jnp.where(o // 32 == i // 32, 1.0, 0.0).astype(BF)

    def natural(source, first, lanes, dests, unroll):
        def one(n, carry):
            c, x = n // 4, n % 4
            block = source[c, x, :, :, :, first : first + lanes * len(dests)].reshape(256, lanes * len(dests))
            found = jnp.dot(permute, block, preferred_element_type=F32).astype(BF)
            for k, dest in enumerate(dests):
                for quarter in range(4):
                    for high in range(2):
                        base = 64 * quarter + 32 * high
                        to = pl.multiple_of(x * 128 + high * 64 + c * 32, 32)
                        dest[pl.ds(to, 32), lanes * quarter : lanes * quarter + lanes] = found[
                            base : base + 32, lanes * k : lanes * k + lanes
                        ]
            return carry

        lax.fori_loop(0, 8, one, 0, unroll=unroll)

    crossed += pass_on(0, qkv, (0,))
    proj = step_xy(1, 1, proj)
    fc = step_xy(2, 1, fc)
    crossed += pass_on(0, qkv, (1, 2))
    crossed_proj = [across(1, flow, 0) for flow in range(2)]
    for copy in crossed:
        copy.wait_recv()
    natural(GQ, 0, 128, [WQ.at[flow] for flow in range(3)], True)

    lane512 = iota((1, 512), 1)
    scale = jnp.zeros((1, 512), F32)
    for head in range(16):
        scale = jnp.where(lane512 // 32 == head, scale_ref[head] * LOG2E, scale)

    def project(image, upper):
        x = X[image, upper].reshape(384, 512)
        for kind in range(3):
            value = jnp.dot(x, WQ[kind], preferred_element_type=F32)
            if kind < 2:
                square = (value * value).astype(BF)
                length = jnp.concatenate(
                    [jnp.dot(square[:, 256 * s : 256 * s + 256], squares, preferred_element_type=F32) for s in range(2)], 1)
                unit = lax.rsqrt(jnp.maximum(length, 1.0))
                value = value * (unit * scale if kind == 0 else unit)
            value = value.astype(BF)
            for j in range(3):
                for block in range(4):
                    QKV[3 * image + j, kind, block, 128 * upper : 128 * upper + 128] = value[
                        128 * j : 128 * j + 128, 128 * block : 128 * block + 128
                    ]

    side = {0: halo[4], 1: halo[7]}
    for image in range(2):
        side[image].wait_recv()
        project(image, image)
    crossed = [across(2, flow, 0) for flow in range(2)]
    crossed_proj += pass_on(1, proj)
    for image in range(2):
        for copy in halo[2 + 3 * image : 4 + 3 * image]:
            copy.wait_recv()
        project(image, 1 - image)

    ones = jnp.ones((256, 128), BF)

    def attend(image, j):
        w = 3 * image + j
        for block in range(4):
            q, k = QKV[w, 0, block], QKV[w, 1, block]
            v = jnp.concatenate([QKV[w, 2, block], ones], 1)
            top = jnp.zeros((256, 128), F32)
            total = jnp.zeros((256, 128), F32)
            for i in range(4):
                here = lane128 // 32 == i
                keep = jnp.where(here, 1.0, 0.0).astype(BF)
                qh = q * keep + FQ[w, i]
                kh = k * keep + FK[w, i]
                score = lax.dot_general(qh, kh, (((1,), (1,)), ((), ())), preferred_element_type=F32)
                weight = jnp.exp2(score + bias[4 * block + i]).astype(BF)
                found = jnp.dot(weight, v, preferred_element_type=F32)
                top = jnp.where(here, found[:, :128], top)
                total = jnp.where(here, found[:, 128:], total)
            M[block] = (top / total).astype(BF)
        mixed = jnp.concatenate([M[b] for b in range(4)], 1)
        done = jnp.dot(mixed, WP[...], preferred_element_type=F32).astype(BF).reshape(2, 2, 64, 512)
        for upper in range(2):
            for right in range(2):
                g = 2 * j + right
                if image == 0 and upper == 0 and g < 5:
                    R[0, 1, g + 1] = done[upper, right]
                elif image == 1 and upper == 1 and g > 0:
                    R[1, 0, g - 1] = done[upper, right]
                else:
                    A[image, upper, g] = done[upper, right]
        back = []
        for right in range(2):
            g = 2 * j + right
            s = 6 * image + g
            if image == 0:
                dst, to = (R.at[0, 0, g + 1], near(1, 0)) if g < 5 else (R.at[0, 0, 0], near(1, 1))
                back.append(send(A.at[0, 1, g], dst, r_send.at[s], r_recv.at[s], to))
                if g == 5:
                    side_back.append(send(A.at[0, 0, 5], R.at[0, 1, 0], r_send.at[12], r_recv.at[12], near(0, 1)))
            else:
                dst, to = (R.at[1, 1, g - 1], near(-1, 0)) if g > 0 else (R.at[1, 1, 5], near(-1, -1))
                back.append(send(A.at[1, 0, g], dst, r_send.at[s], r_recv.at[s], to))
                if g == 0:
                    side_back.append(send(A.at[1, 1, 0], R.at[1, 0, 5], r_send.at[13], r_recv.at[13], near(0, -1)))
        return back

    def second_rows(n, carry):
        c, x = n // 4, n % 4
        for high in range(2):
            for y in range(4):
                to = pl.multiple_of((x * 32 + high * 16 + c * 8 + y * 2) * 16, 32)
                W2[pl.ds(to, 32)] = GF[c, x, y, 2 * high : 2 * high + 2, :, 512:1024].reshape(32, 512)
        return carry

    back = {0: [], 1: []}
    side_back = []
    for copy in crossed_proj:
        copy.wait_recv()
    natural(GP, 0, 128, [WP], True)
    for n, (image, j) in enumerate(((0, 2), (0, 0), (0, 1), (1, 0), (1, 1), (1, 2))):
        back[image] += attend(image, j)
        if n in (2, 3, 4):
            crossed += pass_on(2, fc, (n - 2,))
    for copy in crossed:
        copy.wait_recv()
    natural(GF, 0, 512, [W1], True)
    lax.fori_loop(0, 8, second_rows, 0, unroll=2)

    def mlp(image, half):
        after = T[image, half].reshape(384, 512).astype(F32)
        after = after + layer_norm(R[image, half].reshape(384, 512).astype(F32), gain1_ref[...])
        after = after.astype(BF)
        units = []
        for part in range(4):
            hidden = jnp.dot(after, W1[:, 512 * part : 512 * part + 512], preferred_element_type=F32)
            units.append((0.5 * hidden * (1.0 + lax.erf(hidden * math.sqrt(0.5)))).astype(BF))
        total = jnp.dot(jnp.concatenate(units, 1), W2[...], preferred_element_type=F32)
        result = after.astype(F32) + layer_norm(total, gain2_ref[...])
        result = result.reshape(6, 8, 8, 512)
        O[image, half] = jnp.concatenate([result[g] for g in range(6)], 1).astype(BF)
        copy = pltpu.make_async_copy(O.at[image, half], out_hbm.at[image, 8 * half : 8 * half + 8], out_sem.at[image, half])
        copy.start()
        return copy

    outs = []
    for image in range(2):
        side_back[image].wait_recv()
        outs.append(mlp(image, 1 - image))
        for copy in back[image]:
            copy.wait_recv()
        outs.append(mlp(image, image))
    for copy in sends:
        copy.wait_send()
    for copy in outs:
        copy.wait()


def body(
    tokens, region, w_qkv, w_proj, w_fc1, w_fc2, gain_attn, gain_mlp, table, index, logit_scale
):
    DMA = pltpu.SemaphoreType.DMA
    V = pltpu.VMEM
    tiles = (2, 2, 6, 64, 512)
    return pl.pallas_call(
        kernel,
        out_shape=jax.ShapeDtypeStruct((2, 16, 48, 512), BF),
        in_specs=[pl.BlockSpec(memory_space=pl.ANY)] * 10 + [pl.BlockSpec(memory_space=pltpu.SMEM)],
        out_specs=pl.BlockSpec(memory_space=pl.ANY),
        scratch_shapes=[
            V((16, 48), jnp.int32), V((4, 1536), BF), V((4, 512), BF), V((4, 2048), BF), V((16, 512), BF),
            V((1, 512), F32), V((1, 512), F32), V((16, 961), F32), V((256, 256), jnp.int32),
            V((2, 16, 48, 512), BF), V(tiles, BF), V(tiles, BF), V(tiles, BF), V(tiles, BF), V((2, 2, 8, 48, 512), BF),
            V((2, 4, 4, 4, 16, 384), BF), V((2, 4, 4, 4, 16, 128), BF), V((2, 4, 4, 4, 16, 1024), BF),
            V((3, 512, 512), BF), V((512, 512), BF), V((512, 2048), BF), V((2048, 512), BF),
            V((6, 3, 4, 256, 128), BF), V((4, 256, 128), BF), V((16, 256, 256), F32), V((8, 8, 128), jnp.int32),
            V((3, 16, 128), jnp.int32), V((3, 128, 16), F32), V((256, 128), F32),
            V((6, 4, 256, 128), BF), V((6, 4, 256, 128), BF), V((16, 512), F32),
            DMA((2,)), DMA((9,)), DMA((2, 2)), DMA((3, 3)), DMA((3, 3)), DMA((3, 2, 2, 3)), DMA((3, 2, 2, 3)), DMA((3, 2, 4)), DMA((3, 2, 4)),
            DMA((8,)), DMA((8,)), DMA((14,)), DMA((14,)),
        ],
        compiler_params=pltpu.CompilerParams(
            collective_id=0, has_side_effects=True, vmem_limit_bytes=60 * 1024 * 1024
        ),
    )(
        tokens, region, w_qkv, w_proj, w_fc1, w_fc2,
        gain_attn.reshape(1, 512), gain_mlp.reshape(1, 512), table.T, index, logit_scale,
    )


def solution(mesh):
    split = P(("row", "col"), None)
    return jax.shard_map(
        body,
        mesh=mesh,
        in_specs=(P(None, "row", "col", None), P("row", "col"), split, split, split, split, P(), P(), P(), P(), P()),
        out_specs=P(None, "row", "col", None),
        check_vma=False,
    )
```
